128 devices in a mesh: ctx: 8 (over z, y_hi), shard: 16 (over x, y_lo, core).
Axes of the slice: x: 4, y: 4 (y_hi: 2, y_lo: 2; y = y_hi * 2 + y_lo), z: 4, core: 2. Of those that a mesh axis runs over, the one named last changes fastest.
Arguments:
- inputs: bfloat16 [16, 2048, 1024], P('shard', 'ctx'), may hold values from -6 to 6
- cotangent: bfloat16 [16, 2048, 1024], P('shard', 'ctx'), may hold values from -6 to 6
- w_qkv: bfloat16 [1024, 3072], P('shard'), may hold values from -0.1875 to 0.1875
- bias_query: bfloat16 [1024], P('shard'), may hold values from -4 to 4
- bias_value: bfloat16 [1024], P('shard'), may hold values from -0.3125 to 0.3125
- w_out: bfloat16 [1024, 1024], P('shard'), may hold values from -4 to 4
- bias_out: bfloat16 [1024], P('shard'), may hold values from -4 to 4
- gain_attn: bfloat16 [1024], P('shard'), may hold values from 0.099609375 to 1.8984375
- shift_attn: bfloat16 [1024], P('shard'), may hold values from -4 to 4
- w_up: bfloat16 [1024, 4096], P('shard'), may hold values from -0.1875 to 0.1875
- bias_up: bfloat16 [4096], P('shard'), may hold values from -4 to 4
- w_down: bfloat16 [4096, 1024], P('shard'), may hold values from -0.09375 to 0.09375
- bias_down: bfloat16 [1024], P('shard'), may hold values from -4 to 4
- gain_ffn: bfloat16 [1024], P('shard'), may hold values from 0.099609375 to 1.8984375
- shift_ffn: bfloat16 [1024], P('shard'), may hold values from -4 to 4
Outputs:
- outputs: bfloat16 [16, 2048, 1024], P('shard', 'ctx')
- input_grad: float32 [16, 2048, 1024], P('shard', 'ctx')
- grad_w_qkv: float32 [1024, 3072], P('shard')
- grad_bias_query: float32 [1024], P('shard')
- grad_bias_value: float32 [1024], P('shard')
- grad_w_out: float32 [1024, 1024], P('shard')
- grad_bias_out: float32 [1024], P('shard')
- grad_gain_attn: float32 [1024], P('shard')
- grad_shift_attn: float32 [1024], P('shard')
- grad_w_up: float32 [1024, 4096], P('shard')
- grad_bias_up: float32 [4096], P('shard')
- grad_w_down: float32 [4096, 1024], P('shard')
- grad_bias_down: float32 [1024], P('shard')
- grad_gain_ffn: float32 [1024], P('shard')
- grad_shift_ffn: float32 [1024], P('shard')
The draws below stay inside these ranges and needn't reach their ends.
All inputs are finite; a program needn't handle non-finite values.
Results may differ from the reference program's by a relative error of at most 0.025.
Values may be sent and summed in bfloat16 or wider, within the bound.
No kernel may reach another device: no remote copies, remote signals or barrier semaphores. Data moves between devices by JAX's collectives and lax.ppermute only.
A program may use at most 128 MiB of HBM per device.

```python
import jax
import jax.numpy as jnp
from jax import lax

D = 1024
FF = 4096
HEADS = 16
HD = 64
LEN = 2048
SEQS = 16


def levels(rng, dims, split, least, top_value):
    loudness, own = 1.0, jax.random.fold_in(rng, 6)
    for dim, blocks in split:
        steps = jnp.exp(jax.random.uniform(jax.random.fold_in(own, dim), (blocks,), jnp.float32, least / len(split), top_value / len(split)))
        loudness = loudness * jnp.repeat(steps, dims[dim] // blocks).reshape([-1 if axis == dim else 1 for axis in range(len(dims))])
    return loudness


def centred(rng, dims, scale, most, shards=(), dtype=jnp.bfloat16):
    drawn = jax.random.normal(rng, dims, jnp.float32) * scale
    if len(shards) > 0:
        drawn = levels(rng, dims, shards, -0.22, 0.18) * drawn
    return jnp.clip(drawn, min=-most, max=most).astype(dtype)


def setup_inputs(seed: int = 0) -> dict:
    key_list = jax.random.split(jax.random.key(seed), 16)
    return {
        "inputs": centred(key_list[0], (SEQS, LEN, D), 1.0, 6.0, ((0, 16), (1, 8))),
        "cotangent": centred(key_list[1], (SEQS, LEN, D), 1.0, 6.0, ((0, 16), (1, 8))),
        "w_qkv": centred(key_list[2], (D, 3 * D), D ** -0.5, 0.1875, ((0, 16),)),
        "bias_query": centred(key_list[3], (D,), 0.3, 4.0, ((0, 16),)),
        "bias_value": centred(key_list[4], (D,), 0.02, 0.3125, ((0, 16),)),
        "w_out": centred(key_list[5], (D, D), (max(1, D * 4 // LEN)) ** -0.5, 4.0, ((0, 16),)),
        "bias_out": centred(key_list[6], (D,), 0.3, 4.0, ((0, 16),)),
        "gain_attn": jnp.clip(1.0 + 0.18 * jax.random.normal(key_list[7], (D,), jnp.float32), 0.099609375, 1.8984375).astype(jnp.bfloat16),
        "shift_attn": centred(key_list[8], (D,), 0.3, 4.0, ((0, 16),)),
        "w_up": centred(key_list[9], (D, FF), D ** -0.5, 0.1875, ((0, 16),)),
        "bias_up": centred(key_list[10], (FF,), 0.3, 4.0, ((0, 16),)),
        "w_down": centred(key_list[11], (FF, D), FF ** -0.5, 0.09375, ((0, 16),)),
        "bias_down": centred(key_list[12], (D,), 0.3, 4.0, ((0, 16),)),
        "gain_ffn": jnp.clip(1.0 + 0.18 * jax.random.normal(key_list[13], (D,), jnp.float32), 0.099609375, 1.8984375).astype(jnp.bfloat16),
        "shift_ffn": centred(key_list[14], (D,), 0.3, 4.0, ((0, 16),)),
    }


@jax.custom_vjp
def low(v):
    return lax.optimization_barrier(v.astype(jnp.bfloat16)).astype(jnp.float32)

@jax.custom_vjp
def low_back(v):
    return v

def low_keep(v):
    return (low(v), None)

def low_pass(kept, grad):
    return (grad,)

def back_keep(v):
    return (v, None)

def back_low(kept, grad):
    return (low(grad),)
low.defvjp(low_keep, low_pass)
low_back.defvjp(back_keep, back_low)
ln_epsilon = 1e-12
highest = lax.Precision.HIGHEST

def layer_norm(hidden, norm_gain, norm_shift):
    centered = hidden - lax.optimization_barrier(jnp.mean(hidden, axis=-1, keepdims=True))
    variance = lax.optimization_barrier(jnp.mean(centered * centered, axis=-1, keepdims=True))
    return centered * lax.rsqrt(variance + ln_epsilon) * norm_gain + norm_shift

def product(left, right):
    return jnp.dot(left, right, precision=highest, preferred_element_type=jnp.float32)

def attend_rows(queries, keys, values):
    score_scale = queries.shape[-1] ** (-0.5)
    scores = jnp.einsum('qhe,khe->qhk', queries, keys, precision=highest) * score_scale
    scores = low_back(scores)
    attention = low(jax.nn.softmax(scores, axis=-1))
    return jnp.einsum('qhk,khe->qhe', attention, values, precision=highest)

def encoder_layer(tokens, w_qkv, bias_query, bias_value, w_out, bias_out, gain_attn, shift_attn, w_up, bias_up, w_down, bias_down, gain_ffn, shift_ffn):
    length = tokens.shape[0]
    width = tokens.shape[1]
    bias_all = jnp.concatenate([bias_query, jnp.zeros_like(bias_query), bias_value])
    qkv = low(low_back(product(tokens, w_qkv) + bias_all))
    queries = qkv[:, :width].reshape(length, HEADS, HD)
    keys = qkv[:, width:2 * width].reshape(length, HEADS, HD)
    values = qkv[:, 2 * width:].reshape(length, HEADS, HD)
    block_rows = min(512, length)

    def one_block(query_block):
        return attend_rows(query_block, keys, values)
    attended = lax.map(jax.checkpoint(one_block), queries.reshape(length // block_rows, block_rows, HEADS, HD))
    attended = low(low_back(attended.reshape(length, width)))
    attn = low_back(product(attended, w_out) + bias_out)
    first = layer_norm(tokens + attn, gain_attn, shift_attn)
    pre = low_back(product(low(first), w_up) + bias_up)
    activated = low(jax.nn.gelu(pre, approximate=False))
    ffn = low_back(product(activated, w_down) + bias_down)
    return layer_norm(first + ffn, gain_ffn, shift_ffn)

def reference(inputs, cotangent, w_qkv, bias_query, bias_value, w_out, bias_out, gain_attn, shift_attn, w_up, bias_up, w_down, bias_down, gain_ffn, shift_ffn):
    params = tuple((member.astype(jnp.float32) for member in (w_qkv, bias_query, bias_value, w_out, bias_out, gain_attn, shift_attn, w_up, bias_up, w_down, bias_down, gain_ffn, shift_ffn)))

    def forward(sequences, weights):

        def one_sequence(sequence):
            return encoder_layer(sequence, *weights)
        return lax.map(jax.checkpoint(one_sequence), sequences)
    outputs, pull_back = jax.vjp(forward, inputs.astype(jnp.float32), params)
    input_grad, grads = pull_back(cotangent.astype(jnp.float32))
    return (outputs.astype(jnp.bfloat16), input_grad, grads[0], grads[1], grads[2], grads[3], grads[4], grads[5], grads[6], grads[7], grads[8], grads[9], grads[10], grads[11], grads[12])
```

```python
from functools import partial

import jax
import jax.numpy as jnp
from jax import lax
from jax.experimental import pallas as pl
from jax.experimental.pallas import tpu as pltpu
from jax.sharding import Mesh, PartitionSpec as P

D = 1024
FF = 4096
HEADS = 16
HD = 64
PAIRS = 8
ROWS = 256
LANES = 128
ln_epsilon = 1e-12
F32 = jnp.float32
BF = jnp.bfloat16

ALL = ("z", "yh", "x", "yl", "core")
SHARD = ("x", "yl", "core")
CTX = ("z", "yh")

NN = (((1,), (0,)), ((), ()))
NT = (((1,), (1,)), ((), ()))
TN = (((0,), (0,)), ((), ()))


def dot(left, right, dims=NN):
    return lax.dot_general(left, right, dims, preferred_element_type=F32)


def place(z, y, x, core):
    return (((z % 4 * 2 + y % 4 // 2) * 4 + x % 4) * 2 + y % 2) * 2 + core % 2


def move(array, dz=0, dy=0, dx=0, dcore=0):
    pairs = [
        (place(z, y, x, core), place(z + dz, y + dy, x + dx, core + dcore))
        for z in range(4)
        for y in range(4)
        for x in range(4)
        for core in range(2)
    ]
    return lax.ppermute(array, ALL, pairs)


def plus(*terms):
    total = terms[0].astype(F32)
    for term in terms[1:]:
        total = total + term.astype(F32)
    return total.astype(BF)


def scatter_sum(sent, kept):
    kept = (
        plus(kept[0], move(sent[0], dy=1)),
        plus(kept[1], move(sent[1], dy=-1)),
    )
    ahead = move(kept[0][2], dx=1)
    behind = move(kept[1][2], dx=-1)
    right = (move(plus(kept[0][1], ahead), dx=1), move(kept[1][1], dx=1))
    left = (move(kept[0][3], dx=-1), move(plus(kept[1][3], behind), dx=-1))
    return tuple(plus(kept[h][0], right[h], left[h]) for h in range(2))


def whole(shape):
    return pl.BlockSpec(shape, lambda *_: (0,) * len(shape))


def project_kernel(x_ref, wq_ref, wk_ref, wv_ref, bq_ref, bv_ref, out_ref):
    x = x_ref[...]
    for part, (w_ref, b_ref) in enumerate(((wq_ref, bq_ref), (wk_ref, None), (wv_ref, bv_ref))):
        value = dot(x, w_ref[...])
        if b_ref is not None:
            value = value + b_ref[...]
        low = value.astype(BF)
        out_ref[0, part] = low[:, :LANES]
        out_ref[1, part] = low[:, LANES:]


def project(x, w_qkv, bias_query, bias_value):
    wide = 2 * LANES
    steps = D // wide

    def block(part):
        return pl.BlockSpec((D, wide), lambda b: (0, part * steps + b))

    bias = pl.BlockSpec((1, wide), lambda b: (0, b))
    return pl.pallas_call(
        project_kernel,
        grid=(steps,),
        in_specs=[whole((ROWS, D)), block(0), block(1), block(2), bias, bias],
        out_specs=pl.BlockSpec((2, 3, ROWS, LANES), lambda b: (b, 0, 0, 0)),
        out_shape=jax.ShapeDtypeStruct((PAIRS, 3, ROWS, LANES), BF),
        compiler_params=pltpu.CompilerParams(vmem_limit_bytes=32 << 20),
        cost_estimate=pl.CostEstimate(
            flops=6 * ROWS * D * D, bytes_accessed=8 * D * D, transcendentals=0
        ),
        name="project",
    )(x, w_qkv, w_qkv, w_qkv, bias_query, bias_value)


def attend_kernel(q_ref, k_ref, v_ref, low_ref, full_ref, lse_ref):
    q = q_ref[...] * jnp.asarray(HD**-0.5, BF)
    k = k_ref[...].reshape(-1, LANES)
    v = v_ref[...].reshape(-1, LANES)
    lane = lax.broadcasted_iota(jnp.int32, q.shape, 1)
    outs, logs = [], []
    for h in range(2):
        mine = (lane < HD) if h == 0 else (lane >= HD)
        scores = dot(jnp.where(mine, q, jnp.zeros_like(q)), k, NT)
        peak = jnp.max(scores, axis=1, keepdims=True)
        expo = jnp.exp(scores - peak)
        total = jnp.sum(expo, axis=1, keepdims=True)
        outs.append(dot(expo.astype(BF), v) / total)
        logs.append(peak + jnp.log(total))
    out = jnp.where(lane < HD, outs[0], outs[1])
    full_ref[...] = out
    low_ref[...] = out.astype(BF)
    lse_ref[...] = jnp.where(lane < HD, logs[0], logs[1])


def part_specs():
    block = pl.BlockSpec((None, None, ROWS, LANES), lambda i: (i, 0, 0, 0))
    keys = pl.BlockSpec((PAIRS, None, ROWS, LANES), lambda i: (0, 1, 0, 0))
    values = pl.BlockSpec((PAIRS, None, ROWS, LANES), lambda i: (0, 2, 0, 0))
    return [block, keys, values]


def attend(qkv):
    rows = pl.BlockSpec((None, ROWS, LANES), lambda i: (i, 0, 0))
    shape = (PAIRS, ROWS, LANES)
    n = PAIRS * ROWS
    return pl.pallas_call(
        attend_kernel,
        grid=(PAIRS,),
        in_specs=part_specs(),
        out_specs=[rows, rows, rows],
        out_shape=[
            jax.ShapeDtypeStruct(shape, BF),
            jax.ShapeDtypeStruct(shape, F32),
            jax.ShapeDtypeStruct(shape, F32),
        ],
        compiler_params=pltpu.CompilerParams(vmem_limit_bytes=48 << 20),
        cost_estimate=pl.CostEstimate(
            flops=16 * n * n * LANES, bytes_accessed=16 * n * LANES, transcendentals=2 * n * n
        ),
        name="attend",
    )(qkv, qkv, qkv)


def reflect_kernel(q_ref, k_ref, v_ref, do_ref, o_ref, lse_ref, out_ref, dk_acc, dv_acc):
    i = pl.program_id(0)

    @pl.when(i == 0)
    def _():
        dk_acc[...] = jnp.zeros_like(dk_acc)
        dv_acc[...] = jnp.zeros_like(dv_acc)

    q = q_ref[...] * jnp.asarray(HD**-0.5, BF)
    do = do_ref[...]
    k = k_ref[...].reshape(-1, LANES)
    v = v_ref[...].reshape(-1, LANES)
    lane = lax.broadcasted_iota(jnp.int32, q.shape, 1)
    product = (do.astype(F32) * o_ref[...]).T
    logs = lse_ref[...].T
    dqs, dk, dv = [], None, None
    for h in range(2):
        mine = (lane < HD) if h == 0 else (lane >= HD)
        qh = jnp.where(mine, q, jnp.zeros_like(q))
        doh = jnp.where(mine, do, jnp.zeros_like(do))
        delta = jnp.sum(product[h * HD : (h + 1) * HD], axis=0, keepdims=True)
        probs = jnp.exp(dot(k, qh, NT) - logs[h * HD : h * HD + 1])
        dscores = (probs * (dot(v, doh, NT) - delta)).astype(BF)
        value_part = dot(probs.astype(BF), doh)
        key_part = dot(dscores, qh)
        dv = value_part if dv is None else dv + value_part
        dk = key_part if dk is None else dk + key_part
        dqs.append(dot(dscores, k, TN))
    dk_acc[...] += dk
    dv_acc[...] += dv
    out_ref[i, 0] = (jnp.where(lane < HD, dqs[0], dqs[1]) * HD**-0.5).astype(BF)

    @pl.when(i == PAIRS - 1)
    def _():
        out_ref[:, 1] = dk_acc[...].astype(BF).reshape(PAIRS, ROWS, LANES)
        out_ref[:, 2] = dv_acc[...].astype(BF).reshape(PAIRS, ROWS, LANES)


def reflect(qkv, dattended, attended, logs):
    rows = pl.BlockSpec((None, ROWS, LANES), lambda i: (i, 0, 0))
    n = PAIRS * ROWS
    return pl.pallas_call(
        reflect_kernel,
        grid=(PAIRS,),
        in_specs=part_specs() + [rows, rows, rows],
        out_specs=whole((PAIRS, 3, ROWS, LANES)),
        out_shape=jax.ShapeDtypeStruct((PAIRS, 3, ROWS, LANES), BF),
        scratch_shapes=[pltpu.VMEM((n, LANES), F32)] * 2,
        compiler_params=pltpu.CompilerParams(vmem_limit_bytes=48 << 20),
        cost_estimate=pl.CostEstimate(
            flops=30 * n * n * LANES, bytes_accessed=20 * n * LANES, transcendentals=2 * n * n
        ),
        name="reflect",
    )(qkv, qkv, qkv, dattended, attended, logs)


ACT, DPRE, FIRST, ATT, DFFN, DATTN = 0, FF, 2 * FF, 2 * FF + D, 2 * FF + 2 * D, 2 * FF + 3 * D
PACKED = 2 * FF + 4 * D
TILE = 512
SMALLS = 6


def normalize(hidden):
    centered = hidden - jnp.mean(hidden, axis=-1, keepdims=True)
    deviation = lax.rsqrt(jnp.mean(centered * centered, axis=-1, keepdims=True) + ln_epsilon)
    return centered * deviation, deviation


def norm_back(upstream, normal, deviation, gain):
    scaled = upstream * gain
    return deviation * (
        scaled
        - jnp.mean(scaled, axis=-1, keepdims=True)
        - normal * jnp.mean(scaled * normal, axis=-1, keepdims=True)
    )


def column_sum(value):
    return jnp.sum(value, axis=0, keepdims=True)


def feed_kernel(
    x_ref, cot_ref, att_ref, vec_ref, bup_ref, wout_hbm, wup_hbm, wdown_hbm,
    out_ref, dmixed_ref, datt_ref, pack_ref,
    wout, wup, wdown, first, normal1, slope, total, sems,
):
    copies = [pltpu.make_async_copy(wout_hbm, wout, sems.at[0])]
    ups, downs = [], []
    for t in range(FF // D):
        cols = pl.ds(t * D, D)
        ups.append(pltpu.make_async_copy(wup_hbm.at[:, cols], wup.at[:, cols], sems.at[1 + 2 * t]))
        downs.append(
            pltpu.make_async_copy(wdown_hbm.at[cols, :], wdown.at[cols, :], sems.at[2 + 2 * t])
        )
    copies[0].start()
    for up, down in zip(ups, downs):
        up.start()
        down.start()

    bias_out, gain1, shift1 = vec_ref[2:3], vec_ref[3:4], vec_ref[4:5]
    bias_down, gain2, shift2 = vec_ref[5:6], vec_ref[6:7], vec_ref[7:8]
    att = jnp.concatenate([att_ref[j] for j in range(PAIRS)], axis=1)
    pack_ref[:ROWS, ATT : ATT + D] = att
    copies[0].wait()
    mixed = x_ref[...].astype(F32) + dot(att, wout[...]) + bias_out
    n1, r1 = normalize(mixed)
    normal1[...] = n1
    value = n1 * gain1 + shift1
    first[...] = value
    first_low = value.astype(BF)
    pack_ref[:ROWS, FIRST : FIRST + D] = first_low

    total[...] = value + bias_down
    for t in range(FF // D):
        ups[t].wait()
        downs[t].wait()

        @pl.loop(0, D // TILE)
        def _(u):
            cols = pl.ds(pl.multiple_of(t * D + u * TILE, TILE), TILE)
            pre = dot(pack_ref[:ROWS, FIRST : FIRST + D], wup[:, cols]) + bup_ref[:, cols]
            cdf = 0.5 * (1.0 + lax.erf(pre * 0.7071067811865476))
            slope[:, cols] = cdf + pre * (jnp.exp(-0.5 * pre * pre) * 0.3989422804014327)
            act = (pre * cdf).astype(BF)
            pack_ref[:ROWS, cols] = act
            total[...] += dot(act, wdown[cols, :])

    n2, r2 = normalize(total[...])
    out_ref[...] = (n2 * gain2 + shift2).astype(BF)
    dy = cot_ref[...].astype(F32)
    sums = [None] * SMALLS
    sums[4] = column_sum(dy * n2)
    sums[5] = column_sum(dy)
    dffn = norm_back(dy, n2, r2, gain2)
    dffn_low = dffn.astype(BF)
    pack_ref[:ROWS, DFFN : DFFN + D] = dffn_low
    sums[3] = column_sum(dffn_low.astype(F32))
    total[...] = dffn
    pack_ref[ROWS:, :] = jnp.zeros((16, PACKED), BF)

    @pl.loop(0, FF // TILE)
    def _(u):
        cols = pl.ds(pl.multiple_of(u * TILE, TILE), TILE)
        grads = dot(pack_ref[:ROWS, DFFN : DFFN + D], wdown[cols, :], NT) * slope[:, cols]
        low = grads.astype(BF)
        pack_ref[:ROWS, pl.ds(pl.multiple_of(DPRE + u * TILE, TILE), TILE)] = low
        pack_ref[ROWS:, cols] = jnp.broadcast_to(column_sum(low.astype(F32)), (16, TILE)).astype(BF)
        total[...] += dot(low, wup[:, cols], NT)

    dfirst = total[...]
    n1 = normal1[...]
    sums[1] = column_sum(dfirst * n1)
    sums[2] = column_sum(dfirst)
    dmixed = norm_back(dfirst, n1, r1, gain1)
    dmixed_ref[...] = dmixed
    low = dmixed.astype(BF)
    pack_ref[:ROWS, DATTN : DATTN + D] = low
    sums[0] = column_sum(low.astype(F32))
    for row, value in enumerate(sums):
        pack_ref[ROWS:, FF + row * D : FF + (row + 1) * D] = jnp.broadcast_to(
            value, (16, D)
        ).astype(BF)
    datt = dot(low, wout[...], NT).astype(BF)
    for j in range(PAIRS):
        datt_ref[j] = datt[:, j * LANES : (j + 1) * LANES]


def feed(x, cotangent, attended, vectors, bias_up, w_out, w_up, w_down):
    vmem = pl.BlockSpec(memory_space=pltpu.VMEM)
    hbm = pl.BlockSpec(memory_space=pl.ANY)
    return pl.pallas_call(
        feed_kernel,
        in_specs=[vmem] * 5 + [hbm] * 3,
        out_specs=[vmem] * 4,
        out_shape=[
            jax.ShapeDtypeStruct((ROWS, D), BF),
            jax.ShapeDtypeStruct((ROWS, D), F32),
            jax.ShapeDtypeStruct((PAIRS, ROWS, LANES), BF),
            jax.ShapeDtypeStruct((ROWS + 16, PACKED), BF),
        ],
        scratch_shapes=[
            pltpu.VMEM((D, D), BF),
            pltpu.VMEM((D, FF), BF),
            pltpu.VMEM((FF, D), BF),
            pltpu.VMEM((ROWS, D), F32),
            pltpu.VMEM((ROWS, D), F32),
            pltpu.VMEM((ROWS, FF), F32),
            pltpu.VMEM((ROWS, D), F32),
            pltpu.SemaphoreType.DMA((9,)),
        ],
        compiler_params=pltpu.CompilerParams(vmem_limit_bytes=56 << 20),
        cost_estimate=pl.CostEstimate(
            flops=40 * ROWS * D * D, bytes_accessed=32 * D * D, transcendentals=2 * ROWS * FF
        ),
        name="feed",
    )(x, cotangent, attended, vectors, bias_up, w_out, w_up, w_down)


def pick(ref, base, slot, group):
    block = ref[:, pl.ds(pl.multiple_of(base + slot * 256, 256), 256)]
    out = block[:, :HD]
    for g in range(1, 4):
        out = jnp.where(group == g, block[:, g * HD : (g + 1) * HD], out)
    return out


def pick_all(ref, base, where_x, group):
    return jnp.concatenate(
        [pick(ref, base, lax.rem(where_x + d, 4), group) for d in range(4)], axis=1
    )


HALF_A = 160
HALF_B = 144
HALF_C = 112


def grads_a_kernel(at_ref, own_ref, far_ref, one_ref, two_ref):
    where_x, group = at_ref[0], at_ref[1]

    def product(left, right):
        return dot(left(own_ref), own_ref[:ROWS, right : right + D], TN) + dot(
            left(far_ref), far_ref[:ROWS, right : right + D], TN
        )

    for d in range(4):
        slot = lax.rem(where_x + d, 4) * 4 + group
        value = product(
            lambda ref: ref[:ROWS, pl.ds(pl.multiple_of(slot * 256, 256), 256)], DFFN
        ).astype(BF)
        one_ref[d, :128] = value[:128]
        two_ref[d, :128] = value[128:]
    value = product(
        lambda ref: pick_all(ref.at[:ROWS], ATT, where_x, group), DATTN
    ).astype(BF)
    for d in range(4):
        one_ref[d, 128:160] = value[d * 64 : d * 64 + 32]
        two_ref[d, 128:160] = value[d * 64 + 32 : d * 64 + 64]


def grads_b_kernel(at_ref, own_ref, far_ref, one_ref, two_ref):
    where_x, group = at_ref[0], at_ref[1]
    own = pick_all(own_ref.at[:ROWS], FIRST, where_x, group)
    far = pick_all(far_ref.at[:ROWS], FIRST, where_x, group)
    for block in range(FF // D):
        cols = slice(DPRE + block * D, DPRE + (block + 1) * D)
        value = (
            dot(own, own_ref[:ROWS, cols], TN) + dot(far, far_ref[:ROWS, cols], TN)
        ).astype(BF)
        target = (one_ref, two_ref)[block // 2]
        start = block % 2 * 64
        for d in range(4):
            target[d, start : start + 64] = value[d * 64 : (d + 1) * 64]
    row = lax.broadcasted_iota(jnp.int32, (16, D), 0)
    for d in range(4):
        slot = lax.rem(where_x + d, 4)
        tail = jnp.zeros((16, D), F32)
        cols = pl.ds(pl.multiple_of((slot * 4 + group) * 256, 256), 256)
        for ref in (own_ref, far_ref):
            parts = [ref[ROWS:, cols].astype(F32)]
            for k in range(SMALLS):
                parts.append(pick(ref.at[ROWS:], FF + k * D, slot, group).astype(F32))
            parts.append(jnp.zeros((16, D - 256 - SMALLS * HD), F32))
            tail = tail + jnp.concatenate(parts, axis=1)
        one_ref[d, 128:144] = jnp.where(row == 0, tail, 0.0).astype(BF)
        two_ref[d, 128:144] = jnp.zeros((16, D), BF)


def grads_c_kernel(at_ref, own_x_ref, far_x_ref, own_ref, far_ref, one_ref, two_ref):
    where_x, group = at_ref[0], at_ref[1]
    own = pick_all(own_x_ref, 0, where_x, group)
    far = pick_all(far_x_ref, 0, where_x, group)
    bias = []
    values = []
    for part in range(3):
        mine = jnp.concatenate([own_ref[j, part] for j in range(PAIRS)], axis=1)
        other = jnp.concatenate([far_ref[j, part] for j in range(PAIRS)], axis=1)
        values.append((dot(own, mine, TN) + dot(far, other, TN)).astype(BF))
        if part != 1:
            bias.append(column_sum(mine.astype(F32)) + column_sum(other.astype(F32)))
    row = lax.broadcasted_iota(jnp.int32, (16, D), 0)
    for d in range(4):
        rows = slice(d * 64, (d + 1) * 64)
        low = slice(d * 64, d * 64 + 32)
        high = slice(d * 64 + 32, (d + 1) * 64)
        one_ref[d, :64] = values[0][rows]
        one_ref[d, 64:96] = values[1][low]
        one_ref[d, 96:112] = jnp.zeros((16, D), BF)
        two_ref[d, :32] = values[1][high]
        two_ref[d, 32:96] = values[2][rows]
        slot = lax.rem(where_x + d, 4)
        parts = []
        for vector in bias:
            out = jnp.zeros((1, HD), F32)
            for s in range(16):
                out = jnp.where(slot * 4 + group == s, vector[:, s * HD : (s + 1) * HD], out)
            parts.append(out)
        parts.append(jnp.zeros((1, D - 2 * HD), F32))
        tail = jnp.broadcast_to(jnp.concatenate(parts, axis=1), (16, D))
        two_ref[d, 96:112] = jnp.where(row == 0, tail, 0.0).astype(BF)


def grads(kernel, half, name, flops, at, *arrays):
    vmem = pl.BlockSpec(memory_space=pltpu.VMEM)
    shape = jax.ShapeDtypeStruct((4, half, D), BF)
    return pl.pallas_call(
        kernel,
        in_specs=[pl.BlockSpec(memory_space=pltpu.SMEM)] + [vmem] * len(arrays),
        out_specs=[vmem, vmem],
        out_shape=[shape, shape],
        compiler_params=pltpu.CompilerParams(vmem_limit_bytes=48 << 20),
        cost_estimate=pl.CostEstimate(flops=flops, bytes_accessed=20 << 20, transcendentals=0),
        name=name,
    )(at, *arrays)


def return_kernel(dmixed_ref, grad_ref, w_ref, out_ref):
    step = pl.program_id(0)
    both = jnp.concatenate([grad_ref[0], grad_ref[1]], axis=1)
    value = dot(both, w_ref[...], NT)

    @pl.when(step == 0)
    def _():
        out_ref[...] = dmixed_ref[...] + value

    @pl.when(step > 0)
    def _():
        out_ref[...] += value


def return_input(dmixed, dqkv, w_qkv):
    wide = 2 * LANES
    steps = D // wide
    return pl.pallas_call(
        return_kernel,
        grid=(3 * steps,),
        in_specs=[
            whole((ROWS, D)),
            pl.BlockSpec((2, None, ROWS, LANES), lambda i: (i % steps, i // steps, 0, 0)),
            pl.BlockSpec((D, wide), lambda i: (0, i)),
        ],
        out_specs=whole((ROWS, D)),
        out_shape=jax.ShapeDtypeStruct((ROWS, D), F32),
        compiler_params=pltpu.CompilerParams(vmem_limit_bytes=32 << 20),
        cost_estimate=pl.CostEstimate(
            flops=6 * ROWS * D * D, bytes_accessed=8 * D * D, transcendentals=0
        ),
        name="return_input",
    )(dmixed, dqkv, w_qkv)


def gather(array):
    return lax.all_gather(array, SHARD, axis=0, tiled=True)


def exchange(array):
    return lax.all_to_all(array, CTX, 0, 0, tiled=True)


def shards(
    inputs, cotangent, w_qkv, bias_query, bias_value, w_out, bias_out, gain_attn, shift_attn,
    w_up, bias_up, w_down, bias_down, gain_ffn, shift_ffn,
):
    tokens = inputs[0]
    where_x = lax.axis_index("x").astype(jnp.int32)
    where_y = lax.axis_index("yl").astype(jnp.int32)
    core = lax.axis_index("core").astype(jnp.int32)
    own = jnp.stack([where_x, where_y * 2 + core])
    other = jnp.stack([where_x, (1 - where_y) * 2 + core])

    small = jnp.concatenate(
        [bias_query, bias_value, bias_out, gain_attn, shift_attn, bias_down, gain_ffn, shift_ffn,
         bias_up, jnp.zeros((256,), BF)]
    ).reshape(8, LANES)
    full_small = gather(small).reshape(16, 8 * LANES)
    full_qkv = gather(w_qkv)
    vectors = (
        full_small[:, : 8 * HD].reshape(16, 8, HD).transpose(1, 0, 2).reshape(8, D).astype(F32)
    )
    full_bias_up = full_small[:, 8 * HD : 8 * HD + 256].reshape(1, FF).astype(F32)
    far_tokens = move(tokens, dcore=1)

    qkv = exchange(project(tokens, full_qkv, vectors[0:1], vectors[1:2]))
    full_out = gather(w_out)
    full_up = gather(w_up)
    full_down = gather(w_down)
    attended_low, attended, logs = attend(qkv)
    attended_low = exchange(attended_low)
    outputs, dmixed, dattended, pack = feed(
        tokens, cotangent[0], attended_low, vectors, full_bias_up, full_out, full_up, full_down
    )
    far_pack = move(pack, dcore=1)
    dattended = exchange(dattended)

    flops = 4 * ROWS * D * 2 * D
    sent_a = grads(grads_a_kernel, HALF_A, "grads_a", flops, other, pack, far_pack)
    sent_b = grads(grads_b_kernel, HALF_B, "grads_b", flops, other, pack, far_pack)
    kept_a = grads(grads_a_kernel, HALF_A, "grads_a", flops, own, pack, far_pack)
    kept_b = grads(grads_b_kernel, HALF_B, "grads_b", flops, own, pack, far_pack)
    summed_a = scatter_sum(sent_a, kept_a)
    summed_b = scatter_sum(sent_b, kept_b)

    dqkv = reflect(qkv, dattended, attended, logs)
    dqkv = exchange(dqkv)
    far_dqkv = move(dqkv, dcore=1)
    args = (tokens, far_tokens, dqkv, far_dqkv)
    sent_c = grads(grads_c_kernel, HALF_C, "grads_c", flops, other, *args)
    kept_c = grads(grads_c_kernel, HALF_C, "grads_c", flops, own, *args)
    input_grad = return_input(dmixed, dqkv, full_qkv)
    summed_c = scatter_sum(sent_c, kept_c)

    first_sum = lax.psum_scatter(
        jnp.concatenate(summed_a + summed_b, axis=0), CTX, scatter_dimension=0, tiled=True
    )
    first_sum = lax.all_gather(first_sum, CTX, axis=0, tiled=True).astype(F32)
    last = jnp.concatenate(summed_c, axis=0).reshape(PAIRS, 2 * HALF_C // PAIRS, D)
    last = exchange(last)
    last = jnp.sum(last.astype(F32), axis=0).astype(BF)
    last = lax.all_gather(last, CTX, axis=0, tiled=True).astype(F32)

    a1, a2 = first_sum[:HALF_A], first_sum[HALF_A : 2 * HALF_A]
    b = first_sum[2 * HALF_A :]
    b1, b2 = b[:HALF_B], b[HALF_B:]
    grad_down = jnp.concatenate([a1[:128], a2[:128]], axis=0)
    grad_out = jnp.concatenate([a1[128:160], a2[128:160]], axis=0)
    grad_up = jnp.concatenate([b1[:64], b1[64:128], b2[:64], b2[64:128]], axis=1)
    row = b1[128]
    grad_bias_up = row[:256]
    smalls = [row[256 + k * HD : 256 + (k + 1) * HD] for k in range(SMALLS)]
    c1, c2 = last[:HALF_C], last[HALF_C:]
    grad_qkv = jnp.concatenate(
        [c1[:64], jnp.concatenate([c1[64:96], c2[:32]], axis=0), c2[32:96]], axis=1
    )
    return (
        outputs[None],
        input_grad[None],
        grad_qkv,
        c2[96, :HD],
        c2[96, HD : 2 * HD],
        grad_out,
        smalls[0],
        smalls[1],
        smalls[2],
        grad_up,
        grad_bias_up,
        grad_down,
        smalls[3],
        smalls[4],
        smalls[5],
    )


def solution(mesh):
    fine = Mesh(mesh.devices.reshape(4, 2, 4, 2, 2), ALL)
    tokens = P(SHARD, CTX, None)
    matrix = P(SHARD, None)
    vector = P(SHARD)
    parameters = (
        matrix, vector, vector, matrix, vector, vector, vector,
        matrix, vector, matrix, vector, vector, vector,
    )
    return jax.shard_map(
        shards,
        mesh=fine,
        in_specs=(tokens, tokens) + parameters,
        out_specs=(tokens, tokens) + parameters,
        check_vma=False,
    )
```

```python
from functools import partial

import jax
import jax.numpy as jnp
from jax import lax
from jax.experimental import pallas as pl
from jax.experimental.pallas import tpu as pltpu
from jax.sharding import Mesh, PartitionSpec as P

D = 1024
FF = 4096
HEADS = 16
HD = 64
PAIRS = 8
ROWS = 256
LANES = 128
ln_epsilon = 1e-12
F32 = jnp.float32
BF = jnp.bfloat16

ALL = ("z", "yh", "x", "yl", "core")
SHARD = ("x", "yl", "core")
CTX = ("z", "yh")

NN = (((1,), (0,)), ((), ()))
NT = (((1,), (1,)), ((), ()))
TN = (((0,), (0,)), ((), ()))


def dot(left, right, dims=NN):
    return lax.dot_general(left, right, dims, preferred_element_type=F32)


def place(z, y, x, core):
    return (((z % 4 * 2 + y % 4 // 2) * 4 + x % 4) * 2 + y % 2) * 2 + core % 2


def move(array, dz=0, dy=0, dx=0, dcore=0):
    pairs = [
        (place(z, y, x, core), place(z + dz, y + dy, x + dx, core + dcore))
        for z in range(4)
        for y in range(4)
        for x in range(4)
        for core in range(2)
    ]
    return lax.ppermute(array, ALL, pairs)


def plus(*terms):
    total = terms[0].astype(F32)
    for term in terms[1:]:
        total = total + term.astype(F32)
    return total.astype(BF)


def gather(piece, hold=lambda *arrays: arrays):
    behind = move(piece, dx=1)
    ahead = move(piece, dx=-1)
    side = move(piece, dy=1)
    across = move(behind, dx=1)
    side_behind = move(behind, dy=1)
    side_ahead = move(ahead, dy=-1)
    near = [move(p, dcore=1) for p in (piece, behind, ahead, side)]
    across, side_behind, side_ahead, *near = hold(across, side_behind, side_ahead, *near)
    side_across = move(across, dy=-1)
    last = [across, side_behind, side_ahead, side_across]
    return [piece, behind, ahead, side] + last + near + [move(p, dcore=1) for p in last]


FOUND = [
    (x, y, core)
    for core in range(2)
    for x, y in ((0, 0), (3, 0), (1, 0), (0, 1), (2, 0), (3, 1), (1, 1), (2, 1))
]


def owners(at_ref):
    return [
        (lax.rem(at_ref[0] + x, 4) * 2 + lax.rem(at_ref[1] + y, 2)) * 2
        + lax.rem(at_ref[2] + core, 2)
        for x, y, core in FOUND
    ]


def along_x(halves):
    ahead = move(halves[0][2], dx=1)
    behind = move(halves[1][2], dx=-1)
    right = move(jnp.stack([plus(halves[0][1], ahead), halves[1][1]]), dx=1)
    left = move(jnp.stack([halves[0][3], plus(halves[1][3], behind)]), dx=-1)
    return right, left


def sum_ctx(array):
    parts = exchange(array.reshape(PAIRS, array.shape[0] // PAIRS, D))
    total = jnp.sum(parts.astype(F32), axis=0).astype(BF)
    total = jnp.broadcast_to(total[None], parts.shape)
    return exchange(total).reshape(array.shape).astype(F32)


def whole(shape):
    return pl.BlockSpec(shape, lambda *_: (0,) * len(shape))


EXTRA = 16


def pack_kernel(w_ref, *refs):
    out_ref = refs[-1]
    out_ref[:HD] = w_ref[...]
    parts = [ref[...] for ref in refs[:-1]] + [jnp.zeros((1, 2 * D + 256), BF)]
    row = jnp.concatenate([p.astype(F32) for p in parts], axis=1)
    out_ref[HD:] = jnp.broadcast_to(row, (EXTRA, 3 * D)).astype(BF)


def pack_first(w_qkv, *vectors):
    vmem = pl.BlockSpec(memory_space=pltpu.VMEM)
    return pl.pallas_call(
        pack_kernel,
        in_specs=[vmem] * (1 + len(vectors)),
        out_specs=vmem,
        out_shape=pltpu.HBM((HD + EXTRA, 3 * D), BF),
        name="pack_first",
    )(w_qkv, *[v.reshape(1, -1) for v in vectors])


def project_kernel(at_ref, x_ref, *refs):
    pieces, (out_ref, vec_ref, bup_ref, w, small, sems) = refs[:16], refs[16:]
    copies = []
    for k, (piece, s) in enumerate(zip(pieces, owners(at_ref))):
        copies.append(
            pltpu.make_async_copy(piece.at[pl.ds(HD, EXTRA), pl.ds(0, D)], small.at[s], sems.at[1, k])
        )
        copies.append(pltpu.make_async_copy(piece.at[pl.ds(0, HD)], w.at[s], sems.at[0, k]))
    for copy in copies:
        copy.start()
    for copy in copies:
        copy.wait()
    rows = [small[s].astype(F32)[:1] for s in range(16)]
    for k in range(8):
        vec_ref[k : k + 1] = jnp.concatenate([r[:, k * HD : (k + 1) * HD] for r in rows], axis=1)
    bup_ref[...] = jnp.concatenate([r[:, 8 * HD : 8 * HD + 256] for r in rows], axis=1)
    x = x_ref[...]
    wide = 2 * LANES
    for part in range(3):
        for b in range(D // wide):
            cols = slice(part * D + b * wide, part * D + (b + 1) * wide)
            value = dot(x, w[:, :, cols].reshape(D, wide))
            if part != 1:
                row = 0 if part == 0 else 1
                value = value + vec_ref[row : row + 1, b * wide : (b + 1) * wide]
            low = value.astype(BF)
            out_ref[2 * b, part] = low[:, :LANES]
            out_ref[2 * b + 1, part] = low[:, LANES:]


def project(at, x, pieces):
    vmem = pl.BlockSpec(memory_space=pltpu.VMEM)
    hbm = pl.BlockSpec(memory_space=pltpu.HBM)
    return pl.pallas_call(
        project_kernel,
        in_specs=[pl.BlockSpec(memory_space=pltpu.SMEM), vmem] + [hbm] * 16,
        out_specs=[vmem] * 3,
        out_shape=[
            jax.ShapeDtypeStruct((PAIRS, 3, ROWS, LANES), BF),
            jax.ShapeDtypeStruct((8, D), F32),
            jax.ShapeDtypeStruct((1, FF), F32),
        ],
        scratch_shapes=[
            pltpu.VMEM((16, HD, 3 * D), BF),
            pltpu.VMEM((16, EXTRA, D), BF),
            pltpu.SemaphoreType.DMA((2, 16)),
        ],
        compiler_params=pltpu.CompilerParams(vmem_limit_bytes=32 << 20),
        cost_estimate=pl.CostEstimate(
            flops=6 * ROWS * D * D, bytes_accessed=8 * D * D, transcendentals=0
        ),
        name="project",
    )(at, x, *pieces)


def attend_kernel(q_ref, k_ref, v_ref, low_ref, full_ref, lse_ref):
    q = q_ref[...] * jnp.asarray(HD**-0.5, BF)
    k = k_ref[...].reshape(-1, LANES)
    v = v_ref[...].reshape(-1, LANES)
    lane = lax.broadcasted_iota(jnp.int32, q.shape, 1)
    outs, logs = [], []
    for h in range(2):
        mine = (lane < HD) if h == 0 else (lane >= HD)
        scores = dot(jnp.where(mine, q, jnp.zeros_like(q)), k, NT)
        peak = jnp.max(scores, axis=1, keepdims=True)
        expo = jnp.exp(scores - peak)
        total = jnp.sum(expo, axis=1, keepdims=True)
        outs.append(dot(expo.astype(BF), v) / total)
        logs.append(peak + jnp.log(total))
    out = jnp.where(lane < HD, outs[0], outs[1])
    full_ref[...] = out
    low_ref[...] = out.astype(BF)
    lse_ref[...] = jnp.where(lane < HD, logs[0], logs[1])


def part_specs():
    block = pl.BlockSpec((None, None, ROWS, LANES), lambda i: (i, 0, 0, 0))
    keys = pl.BlockSpec((PAIRS, None, ROWS, LANES), lambda i: (0, 1, 0, 0))
    values = pl.BlockSpec((PAIRS, None, ROWS, LANES), lambda i: (0, 2, 0, 0))
    return [block, keys, values]


def attend(qkv):
    rows = pl.BlockSpec((None, ROWS, LANES), lambda i: (i, 0, 0))
    shape = (PAIRS, ROWS, LANES)
    n = PAIRS * ROWS
    return pl.pallas_call(
        attend_kernel,
        grid=(PAIRS,),
        in_specs=part_specs(),
        out_specs=[rows, rows, rows],
        out_shape=[
            jax.ShapeDtypeStruct(shape, BF),
            jax.ShapeDtypeStruct(shape, F32),
            jax.ShapeDtypeStruct(shape, F32),
        ],
        compiler_params=pltpu.CompilerParams(vmem_limit_bytes=48 << 20),
        cost_estimate=pl.CostEstimate(
            flops=16 * n * n * LANES, bytes_accessed=16 * n * LANES, transcendentals=2 * n * n
        ),
        name="attend",
    )(qkv, qkv, qkv)


def reflect_kernel(q_ref, k_ref, v_ref, do_ref, o_ref, lse_ref, out_ref, dk_acc, dv_acc):
    i = pl.program_id(0)

    @pl.when(i == 0)
    def _():
        dk_acc[...] = jnp.zeros_like(dk_acc)
        dv_acc[...] = jnp.zeros_like(dv_acc)

    q = q_ref[...] * jnp.asarray(HD**-0.5, BF)
    do = do_ref[...]
    k = k_ref[...].reshape(-1, LANES)
    v = v_ref[...].reshape(-1, LANES)
    lane = lax.broadcasted_iota(jnp.int32, q.shape, 1)
    product = (do.astype(F32) * o_ref[...]).T
    logs = lse_ref[...].T
    dqs, dk, dv = [], None, None
    for h in range(2):
        mine = (lane < HD) if h == 0 else (lane >= HD)
        qh = jnp.where(mine, q, jnp.zeros_like(q))
        doh = jnp.where(mine, do, jnp.zeros_like(do))
        delta = jnp.sum(product[h * HD : (h + 1) * HD], axis=0, keepdims=True)
        probs = jnp.exp(dot(k, qh, NT) - logs[h * HD : h * HD + 1])
        dscores = (probs * (dot(v, doh, NT) - delta)).astype(BF)
        value_part = dot(probs.astype(BF), doh)
        key_part = dot(dscores, qh)
        dv = value_part if dv is None else dv + value_part
        dk = key_part if dk is None else dk + key_part
        dqs.append(dot(dscores, k, TN))
    dk_acc[...] += dk
    dv_acc[...] += dv
    out_ref[i, 0] = (jnp.where(lane < HD, dqs[0], dqs[1]) * HD**-0.5).astype(BF)

    @pl.when(i == PAIRS - 1)
    def _():
        out_ref[:, 1] = dk_acc[...].astype(BF).reshape(PAIRS, ROWS, LANES)
        out_ref[:, 2] = dv_acc[...].astype(BF).reshape(PAIRS, ROWS, LANES)


def reflect(qkv, dattended, attended, logs):
    rows = pl.BlockSpec((None, ROWS, LANES), lambda i: (i, 0, 0))
    n = PAIRS * ROWS
    return pl.pallas_call(
        reflect_kernel,
        grid=(PAIRS,),
        in_specs=part_specs() + [rows, rows, rows],
        out_specs=whole((PAIRS, 3, ROWS, LANES)),
        out_shape=jax.ShapeDtypeStruct((PAIRS, 3, ROWS, LANES), BF),
        scratch_shapes=[pltpu.VMEM((n, LANES), F32)] * 2,
        compiler_params=pltpu.CompilerParams(vmem_limit_bytes=48 << 20),
        cost_estimate=pl.CostEstimate(
            flops=30 * n * n * LANES, bytes_accessed=20 * n * LANES, transcendentals=2 * n * n
        ),
        name="reflect",
    )(qkv, qkv, qkv, dattended, attended, logs)


ACT, DPRE, FIRST, ATT, DFFN, DATTN = 0, FF, 2 * FF, 2 * FF + D, 2 * FF + 2 * D, 2 * FF + 3 * D
PACKED = 2 * FF + 4 * D
TILE = 512
SMALLS = 6
SMALL = D + SMALLS * 256


def by_group(value, width):
    cut = [value[:, i * width : (i + 1) * width] for i in range(16)]
    return jnp.concatenate([cut[x * 4 + g] for g in range(4) for x in range(4)], axis=1)


def normalize(hidden):
    centered = hidden - jnp.mean(hidden, axis=-1, keepdims=True)
    deviation = lax.rsqrt(jnp.mean(centered * centered, axis=-1, keepdims=True) + ln_epsilon)
    return centered * deviation, deviation


def norm_back(upstream, normal, deviation, gain):
    scaled = upstream * gain
    return deviation * (
        scaled
        - jnp.mean(scaled, axis=-1, keepdims=True)
        - normal * jnp.mean(scaled * normal, axis=-1, keepdims=True)
    )


def column_sum(value):
    return jnp.sum(value, axis=0, keepdims=True)


def feed_kernel(
    at_ref, x_ref, cot_ref, att_ref, vec_ref, bup_ref, *refs
):
    pieces = refs[:16]
    out_ref, dmixed_ref, datt_ref, pack_ref = refs[16:20]
    feed_body(
        owners(at_ref), pieces, x_ref, cot_ref, att_ref, vec_ref, bup_ref,
        out_ref, dmixed_ref, datt_ref, pack_ref, *refs[20:],
    )


def feed_body(
    places, pieces, x_ref, cot_ref, att_ref, vec_ref, bup_ref,
    out_ref, dmixed_ref, datt_ref, pack_ref,
    wout, wup, wdown, first, low_first, normal1, slope, total, bias_sum, sems,
):
    outs, ups, downs = [], [], []
    for k, (piece, s) in enumerate(zip(pieces, places)):
        outs.append(pltpu.make_async_copy(piece.at[0], wout.at[s], sems.at[0, k]))
        ups.append(pltpu.make_async_copy(piece.at[pl.ds(1, 4)], wup.at[:, s], sems.at[1, k]))
        downs.append(pltpu.make_async_copy(piece.at[pl.ds(5, 4)], wdown.at[s], sems.at[2, k]))
    for copy in outs + ups + downs:
        copy.start()

    bias_out, gain1, shift1 = vec_ref[2:3], vec_ref[3:4], vec_ref[4:5]
    bias_down, gain2, shift2 = vec_ref[5:6], vec_ref[6:7], vec_ref[7:8]
    att = jnp.concatenate([att_ref[j] for j in range(PAIRS)], axis=1)
    pack_ref[:ROWS, ATT : ATT + D] = by_group(att, HD)
    for copy in outs:
        copy.wait()
    mixed = x_ref[...].astype(F32) + dot(att, wout[...].reshape(D, D)) + bias_out
    n1, r1 = normalize(mixed)
    normal1[...] = n1
    value = n1 * gain1 + shift1
    first[...] = value
    first_low = value.astype(BF)
    low_first[...] = first_low
    pack_ref[:ROWS, FIRST : FIRST + D] = by_group(first_low, HD)

    total[...] = value + bias_down
    for copy in ups + downs:
        copy.wait()

    def up_tile(u):
        part = pl.ds(pl.multiple_of(u % 2 * TILE, TILE), TILE)
        return wup[u // 2, :, :, part].reshape(D, TILE)

    def down_tile(u):
        return wdown[pl.ds(u * 2, 2)].reshape(TILE, D)

    @pl.loop(0, FF // TILE)
    def _(u):
        cols = pl.ds(pl.multiple_of(u * TILE, TILE), TILE)
        pre = dot(low_first[...], up_tile(u)) + bup_ref[:, cols]
        cdf = 0.5 * (1.0 + lax.erf(pre * 0.7071067811865476))
        slope[:, cols] = cdf + pre * (jnp.exp(-0.5 * pre * pre) * 0.3989422804014327)
        act = (pre * cdf).astype(BF)
        pack_ref[:ROWS, cols] = act
        total[...] += dot(act, down_tile(u))

    n2, r2 = normalize(total[...])
    out_ref[...] = (n2 * gain2 + shift2).astype(BF)
    dy = cot_ref[...].astype(F32)
    sums = [None] * SMALLS
    sums[4] = column_sum(dy * n2)
    sums[5] = column_sum(dy)
    dffn = norm_back(dy, n2, r2, gain2)
    dffn_low = dffn.astype(BF)
    pack_ref[:ROWS, DFFN : DFFN + D] = dffn_low
    sums[3] = column_sum(dffn_low.astype(F32))
    total[...] = dffn
    pack_ref[ROWS:, :] = jnp.zeros((16, PACKED), BF)

    @pl.loop(0, FF // TILE)
    def _(u):
        cols = pl.ds(pl.multiple_of(u * TILE, TILE), TILE)
        grads = dot(pack_ref[:ROWS, DFFN : DFFN + D], down_tile(u), NT) * slope[:, cols]
        low = grads.astype(BF)
        pack_ref[:ROWS, pl.ds(pl.multiple_of(DPRE + u * TILE, TILE), TILE)] = low
        bias_sum[:, cols] = column_sum(low.astype(F32))
        total[...] += dot(low, up_tile(u), NT)

    dfirst = total[...]
    n1 = normal1[...]
    sums[1] = column_sum(dfirst * n1)
    sums[2] = column_sum(dfirst)
    dmixed = norm_back(dfirst, n1, r1, gain1)
    dmixed_ref[...] = dmixed
    low = dmixed.astype(BF)
    pack_ref[:ROWS, DATTN : DATTN + D] = low
    sums[0] = column_sum(low.astype(F32))
    sums = [by_group(value, HD) for value in sums]
    ups = by_group(bias_sum[...], 256)
    for g in range(4):
        parts = [ups[:, g * D : (g + 1) * D]] + [v[:, g * 256 : (g + 1) * 256] for v in sums]
        pack_ref[ROWS:, g * SMALL : (g + 1) * SMALL] = jnp.broadcast_to(
            jnp.concatenate(parts, axis=1), (16, SMALL)
        ).astype(BF)
    datt = dot(low, wout[...].reshape(D, D), NT).astype(BF)
    for j in range(PAIRS):
        datt_ref[j] = datt[:, j * LANES : (j + 1) * LANES]


def feed(at, x, cotangent, attended, vectors, bias_up, pieces):
    vmem = pl.BlockSpec(memory_space=pltpu.VMEM)
    hbm = pl.BlockSpec(memory_space=pltpu.HBM)
    return pl.pallas_call(
        feed_kernel,
        in_specs=[pl.BlockSpec(memory_space=pltpu.SMEM)] + [vmem] * 5 + [hbm] * 16,
        out_specs=[vmem] * 4,
        out_shape=[
            jax.ShapeDtypeStruct((ROWS, D), BF),
            jax.ShapeDtypeStruct((ROWS, D), F32),
            jax.ShapeDtypeStruct((PAIRS, ROWS, LANES), BF),
            jax.ShapeDtypeStruct((ROWS + 16, PACKED), BF),
        ],
        scratch_shapes=[
            pltpu.VMEM((16, HD, D), BF),
            pltpu.VMEM((4, 16, HD, D), BF),
            pltpu.VMEM((16, 4, HD, D), BF),
            pltpu.VMEM((ROWS, D), F32),
            pltpu.VMEM((ROWS, D), BF),
            pltpu.VMEM((ROWS, D), F32),
            pltpu.VMEM((ROWS, FF), F32),
            pltpu.VMEM((ROWS, D), F32),
            pltpu.VMEM((1, FF), F32),
            pltpu.SemaphoreType.DMA((3, 16)),
        ],
        compiler_params=pltpu.CompilerParams(vmem_limit_bytes=56 << 20),
        cost_estimate=pl.CostEstimate(
            flops=40 * ROWS * D * D, bytes_accessed=32 * D * D, transcendentals=2 * ROWS * FF
        ),
        name="feed",
    )(at, x, cotangent, attended, vectors, bias_up, *pieces)


HALF_A = 160
HALF_B = 144


def slot_of(at_ref, x):
    return lax.rem(x + 4 - at_ref[0], 4)


def both_cores(own, far):
    return jnp.concatenate([own[...], far[...]], axis=0)


def grads_a_kernel(at_ref, *refs):
    step = pl.program_id(0)
    act, att, dffn, dattn = (both_cores(*pair) for pair in zip(refs[:4], refs[4:8]))
    one, two = refs[8:]
    value = dot(act, dffn, TN).astype(BF)
    slot = slot_of(at_ref, step)
    one[slot, :128] = value[:128]
    two[slot, :128] = value[128:]

    @pl.when(step == 0)
    def _():
        value = dot(att, dattn, TN).astype(BF)
        for x in range(4):
            one[slot_of(at_ref, x), 128:160] = value[x * 64 : x * 64 + 32]
            two[slot_of(at_ref, x), 128:160] = value[x * 64 + 32 : x * 64 + 64]


def grads_b_kernel(at_ref, *refs):
    step = pl.program_id(0)
    first, first_other, dpre, row_own, row_other = (
        both_cores(*pair) for pair in zip(refs[:5], refs[5:10])
    )
    one, two = refs[10:]
    value = dot(jnp.concatenate([first, first_other], axis=1), dpre, TN).astype(BF)
    for half, target in enumerate((one, two)):

        @pl.when(step // 2 == half)
        def _():
            start = pl.multiple_of(step % 2 * 64, 64)
            for side in range(2):
                for x in range(4):
                    rows = value[(side * 4 + x) * 64 : (side * 4 + x + 1) * 64]
                    target[slot_of(at_ref, x), side, pl.ds(start, 64)] = rows

    @pl.when(step == 0)
    def _():
        row = lax.broadcasted_iota(jnp.int32, (16, D), 0)
        for side, tail in enumerate((row_own, row_other)):
            tail = tail[:16].astype(F32) + tail[16:].astype(F32)
            for x in range(4):
                parts = [tail[:, x * 256 : (x + 1) * 256]]
                for k in range(SMALLS):
                    start = D + k * 256 + x * HD
                    parts.append(tail[:, start : start + HD])
                parts.append(jnp.zeros((16, D - 256 - SMALLS * HD), F32))
                value = jnp.where(row == 0, jnp.concatenate(parts, axis=1), 0.0)
                one[slot_of(at_ref, x), side, 128:144] = value.astype(BF)
                two[slot_of(at_ref, x), side, 128:144] = jnp.zeros((16, D), BF)


def columns(width, where):
    return pl.BlockSpec((ROWS, width), lambda i, at: (0, where(i, at)))


def small_row(where):
    return pl.BlockSpec((16, SMALL), lambda i, at: (ROWS // 16, where(at)))


def grads(kernel, specs, shape, name, at, pack, far_pack):
    return pl.pallas_call(
        kernel,
        grid_spec=pltpu.PrefetchScalarGridSpec(
            num_scalar_prefetch=1,
            grid=(4,),
            in_specs=specs + specs,
            out_specs=[whole(shape)] * 2,
        ),
        out_shape=[pltpu.HBM(shape, BF)] * 2,
        compiler_params=pltpu.CompilerParams(vmem_limit_bytes=48 << 20),
        cost_estimate=pl.CostEstimate(
            flops=6 * ROWS * D * D, bytes_accessed=12 << 20, transcendentals=0
        ),
        name=name,
    )(at, *([pack] * len(specs)), *([far_pack] * len(specs)))


def grads_a(at, pack, far_pack):
    specs = [
        columns(256, lambda i, at: i * 4 + at[1]),
        columns(256, lambda i, at: ATT // 256 + at[1]),
        columns(D, lambda i, at: DFFN // D),
        columns(D, lambda i, at: DATTN // D),
    ]
    return grads(grads_a_kernel, specs, (4, HALF_A, D), "grads_a", at, pack, far_pack)


def grads_b(at, pack, far_pack):
    specs = [
        columns(256, lambda i, at: FIRST // 256 + at[1]),
        columns(256, lambda i, at: FIRST // 256 + at[2]),
        columns(D, lambda i, at: DPRE // D + i),
        small_row(lambda at: at[1]),
        small_row(lambda at: at[2]),
    ]
    return grads(grads_b_kernel, specs, (4, 2, HALF_B, D), "grads_b", at, pack, far_pack)


def grads_qkv_kernel(x_ref, g_ref, out_ref, total, sums):
    step = pl.program_id(0)

    @pl.when(step == 0)
    def _():
        total[...] = jnp.zeros_like(total)
        sums[...] = jnp.zeros_like(sums)

    both = jnp.concatenate([g_ref[part] for part in range(3)], axis=1)
    total[...] += dot(both, x_ref[...], TN)
    sums[...] += jnp.broadcast_to(column_sum(both.astype(F32)), sums.shape)

    @pl.when(step == PAIRS - 1)
    def _():
        value = total[...].T.astype(BF)
        for s in range(16):
            out_ref[s, :HD] = value[s * HD : (s + 1) * HD]
            out_ref[s, HD:] = sums[...].astype(BF)


def grads_qkv(x_all, dqkv):
    wide = 3 * LANES
    return pl.pallas_call(
        grads_qkv_kernel,
        grid=(PAIRS,),
        in_specs=[
            pl.BlockSpec((None, ROWS, D), lambda i: (i, 0, 0)),
            pl.BlockSpec((None, 3, ROWS, LANES), lambda i: (i, 0, 0, 0)),
        ],
        out_specs=whole((16, HD + 16, wide)),
        out_shape=jax.ShapeDtypeStruct((16, HD + 16, wide), BF),
        scratch_shapes=[pltpu.VMEM((wide, D), F32), pltpu.VMEM((16, wide), F32)],
        compiler_params=pltpu.CompilerParams(vmem_limit_bytes=32 << 20),
        cost_estimate=pl.CostEstimate(
            flops=6 * ROWS * D * D, bytes_accessed=6 << 20, transcendentals=0
        ),
        name="grads_qkv",
    )(x_all, dqkv)


def return_kernel(at_ref, dmixed_ref, grad_ref, *refs):
    pieces, (out_ref, w, sems) = refs[:16], refs[16:]
    copies = [
        pltpu.make_async_copy(piece.at[pl.ds(0, HD)], w.at[s], sems.at[k])
        for k, (piece, s) in enumerate(zip(pieces, owners(at_ref)))
    ]
    for copy in copies:
        copy.start()
    for copy in copies:
        copy.wait()
    out_ref[...] = dmixed_ref[...]
    for part in range(3):
        for b in range(2):
            both = jnp.concatenate([grad_ref[4 * b + j, part] for j in range(4)], axis=1)
            cols = slice(part * D + b * TILE, part * D + (b + 1) * TILE)
            out_ref[...] += dot(both, w[:, :, cols].reshape(D, TILE), NT)


def return_input(at, dmixed, dqkv, pieces):
    vmem = pl.BlockSpec(memory_space=pltpu.VMEM)
    hbm = pl.BlockSpec(memory_space=pltpu.HBM)
    return pl.pallas_call(
        return_kernel,
        in_specs=[pl.BlockSpec(memory_space=pltpu.SMEM), vmem, vmem] + [hbm] * 16,
        out_specs=vmem,
        out_shape=jax.ShapeDtypeStruct((ROWS, D), F32),
        scratch_shapes=[pltpu.VMEM((16, HD, 3 * D), BF), pltpu.SemaphoreType.DMA((16,))],
        compiler_params=pltpu.CompilerParams(vmem_limit_bytes=32 << 20),
        cost_estimate=pl.CostEstimate(
            flops=6 * ROWS * D * D, bytes_accessed=8 * D * D, transcendentals=0
        ),
        name="return_input",
    )(at, dmixed, dqkv, *pieces)


def exchange(array):
    return lax.all_to_all(array, CTX, 0, 0, tiled=True)


def shards(
    inputs, cotangent, w_qkv, bias_query, bias_value, w_out, bias_out, gain_attn, shift_attn,
    w_up, bias_up, w_down, bias_down, gain_ffn, shift_ffn,
):
    tokens = inputs[0]
    where_x = lax.axis_index("x").astype(jnp.int32)
    where_y = lax.axis_index("yl").astype(jnp.int32)
    core = lax.axis_index("core").astype(jnp.int32)
    at = jnp.stack([where_x, where_y, core])
    group, group_other = where_y * 2 + core, (1 - where_y) * 2 + core
    own = jnp.stack([where_x, group, group_other])
    other = jnp.stack([where_x, group_other, group])
    barrier = lax.optimization_barrier

    first_piece = pack_first(
        w_qkv, bias_query, bias_value, bias_out, gain_attn, shift_attn, bias_down, gain_ffn,
        shift_ffn, bias_up,
    )
    first_pieces = gather(first_piece)
    piece = jnp.concatenate(
        [w_out[None], w_up.reshape(HD, 4, D).transpose(1, 0, 2), w_down.reshape(4, HD, D)], axis=0
    )
    piece, *first_pieces[1:3] = barrier((piece, *first_pieces[1:3]))

    far = move(tokens, dy=2)
    both = jnp.where(lax.axis_index("yh") == 0, jnp.stack([tokens, far]), jnp.stack([far, tokens]))
    both, tokens = barrier((both, tokens))
    x_all = lax.all_gather(both, "z", axis=0, tiled=True)

    qkv, vectors, full_bias_up = project(at, tokens, first_pieces)
    qkv = exchange(qkv)
    attended_low, attended, logs = attend(qkv)
    held = []

    def hold(*arrays):
        out = barrier((*arrays, attended_low))
        held.append(out[-1])
        return out[:-1]

    pieces = gather(piece, hold)
    attended_low = exchange(held[0])
    x_all, attended_low = barrier((x_all, attended_low))
    outputs, dmixed, dattended, pack = feed(
        at, tokens, cotangent[0], attended_low, vectors, full_bias_up, pieces
    )
    far_pack = move(pack, dcore=1)
    dattended = exchange(dattended)

    b_halves = grads_b(own, pack, far_pack)
    a_sent = grads_a(other, pack, far_pack)
    a_arrived = tuple(move(a_sent[h], dy=1 - 2 * h) for h in range(2))
    a_kept = grads_a(own, pack, far_pack)
    b_right, b_left = along_x(b_halves)
    dqkv = reflect(qkv, dattended, attended, logs)
    a_arrived, b_right, b_left, dqkv = barrier((a_arrived, b_right, b_left, dqkv))

    b_sum = [plus(b_halves[h][0], b_right[h], b_left[h]) for h in range(2)]
    b_sum = [
        plus(b_sum[h][0], move(b_sum[h][1], dy=1 - 2 * h)) for h in range(2)
    ]
    a_halves = [plus(a_kept[h], a_arrived[h]) for h in range(2)]
    a_right, a_left = along_x(a_halves)
    b_sum = sum_ctx(jnp.concatenate(b_sum, axis=0))

    part = grads_qkv(x_all, dqkv)
    dqkv = exchange(dqkv)
    part, dqkv = barrier((part, dqkv))
    part = lax.all_to_all(part, SHARD, 0, 0, tiled=True)
    part = jnp.sum(part.astype(F32), axis=0).astype(BF)
    part = jnp.broadcast_to(part[None], (PAIRS,) + part.shape)
    part = exchange(part).astype(F32)
    input_grad = return_input(at, dmixed, dqkv, first_pieces)

    a_sum = [plus(a_halves[h][0], a_right[h], a_left[h]) for h in range(2)]
    a_sum = sum_ctx(jnp.concatenate(a_sum, axis=0))

    a1, a2 = a_sum[:HALF_A], a_sum[HALF_A:]
    b1, b2 = b_sum[:HALF_B], b_sum[HALF_B:]
    grad_down = jnp.concatenate([a1[:128], a2[:128]], axis=0)
    grad_out = jnp.concatenate([a1[128:160], a2[128:160]], axis=0)
    grad_up = jnp.concatenate([b1[:64], b1[64:128], b2[:64], b2[64:128]], axis=1)
    row = b1[128]
    grad_bias_up = row[:256]
    smalls = [row[256 + k * HD : 256 + (k + 1) * HD] for k in range(SMALLS)]
    rows = part[:, :HD].reshape(PAIRS, HD, 3, LANES).transpose(1, 2, 0, 3)
    grad_qkv = rows.reshape(HD, 3 * D)
    shard = where_x * 4 + where_y * 2 + core
    sums = part[:, HD].reshape(PAIRS, 3, 2, HD)
    mine = lax.dynamic_index_in_dim(sums, shard // 2, 0, keepdims=False)
    mine = lax.dynamic_index_in_dim(mine, shard % 2, 1, keepdims=False)
    return (
        outputs[None],
        input_grad[None],
        grad_qkv,
        mine[0],
        mine[2],
        grad_out,
        smalls[0],
        smalls[1],
        smalls[2],
        grad_up,
        grad_bias_up,
        grad_down,
        smalls[3],
        smalls[4],
        smalls[5],
    )


def solution(mesh):
    fine = Mesh(mesh.devices.reshape(4, 2, 4, 2, 2), ALL)
    tokens = P(SHARD, CTX, None)
    matrix = P(SHARD, None)
    vector = P(SHARD)
    parameters = (
        matrix, vector, vector, matrix, vector, vector, vector,
        matrix, vector, matrix, vector, vector, vector,
    )
    return jax.shard_map(
        shards,
        mesh=fine,
        in_specs=(tokens, tokens) + parameters,
        out_specs=(tokens, tokens) + parameters,
        check_vma=False,
    )
```

```python
from functools import partial

import jax
import jax.numpy as jnp
from jax import lax
from jax.experimental import pallas as pl
from jax.experimental.pallas import tpu as pltpu
from jax.sharding import Mesh, PartitionSpec as P

D = 1024
FF = 4096
HEADS = 16
HD = 64
PAIRS = 8
ROWS = 256
LANES = 128
ln_epsilon = 1e-12
VMEM_LIMIT = 60 << 20
SHARE = 1
F32 = jnp.float32
BF = jnp.bfloat16

ALL = ("z", "yh", "x", "yl", "core")
SHARD = ("x", "yl", "core")
CTX = ("z", "yh")

NN = (((1,), (0,)), ((), ()))
NT = (((1,), (1,)), ((), ()))
TN = (((0,), (0,)), ((), ()))


def dot(left, right, dims=NN):
    return lax.dot_general(left, right, dims, preferred_element_type=F32)


def place(z, y, x, core):
    return (((z % 4 * 2 + y % 4 // 2) * 4 + x % 4) * 2 + y % 2) * 2 + core % 2


def move(array, dz=0, dy=0, dx=0, dcore=0):
    pairs = [
        (place(z, y, x, core), place(z + dz, y + dy, x + dx, core + dcore))
        for z in range(4)
        for y in range(4)
        for x in range(4)
        for core in range(2)
    ]
    return lax.ppermute(array, ALL, pairs)


def plus(*terms):
    total = terms[0].astype(F32)
    for term in terms[1:]:
        total = total + term.astype(F32)
    return total.astype(BF)


def gather(piece, way, after_two=None, hold=None, hold_last=None):
    barrier = lax.optimization_barrier
    behind, ahead, side = barrier((move(piece, dx=1), move(piece, dx=-1), move(piece, dy=way)))
    across = move(behind, dx=1)
    side_behind = move(behind, dy=-way)
    side_ahead = move(side, dx=-1)
    near = [move(p, dcore=1) for p in (piece, behind, ahead)]
    if hold is None:
        across, side_behind, side_ahead, *near = barrier((across, side_behind, side_ahead, *near))
        after_two.append(across)
        side_across = move(across, dy=way)
        late = (side, across, side_behind, side_ahead, side_across)
        side, *last = late = barrier(late)
        near += [move(p, dcore=1) for p in late]
    else:
        near.append(move(side, dcore=1))
        side_across = move(across, dy=way)
        side_behind, side_ahead, *near = hold(near, side_behind, side_ahead)
        last = [across, side_behind, side_ahead, side_across]
        near += [move(p, dcore=1) for p in last[:3]]
        near.append(move(hold_last(side_across), dcore=1))
    return [piece, behind, ahead, side] + last + near


FOUND = [
    (x, y, core)
    for core in range(2)
    for x, y in ((0, 0), (3, 0), (1, 0), (0, 1), (2, 0), (3, 1), (1, 1), (2, 1))
]


def owners(at_ref):
    return [
        (lax.rem(at_ref[0] + x, 4) * 2 + lax.rem(at_ref[1] + y, 2)) * 2
        + lax.rem(at_ref[2] + core, 2)
        for x, y, core in FOUND
    ]


def along_x(halves, hold, across=None):
    def slot(half, d, *more):
        return plus(*[term[d] for term in halves[half]], *more)

    across = across or (slot(0, 2), slot(1, 2))
    ahead, behind = hold(move(across[0], dx=1), move(across[1], dx=-1))
    right = move(jnp.stack([slot(0, 1, ahead), slot(1, 1)]), dx=1)
    left = move(jnp.stack([slot(0, 3), slot(1, 3, behind)]), dx=-1)
    return right, left


def cost(flops, bytes_accessed, transcendentals):
    return pl.CostEstimate(
        flops=flops // SHARE,
        bytes_accessed=bytes_accessed // SHARE,
        transcendentals=transcendentals // SHARE,
    )


def whole(shape):
    return pl.BlockSpec(shape, lambda *_: (0,) * len(shape))


EXTRA = 16


def pack_kernel(w_ref, *refs):
    out_ref = refs[-1]
    out_ref[:HD] = w_ref[...]
    parts = [ref[...] for ref in refs[:-1]] + [jnp.zeros((1, 2 * D + 256), BF)]
    row = jnp.concatenate([p.astype(F32) for p in parts], axis=1)
    out_ref[HD:] = jnp.broadcast_to(row, (EXTRA, 3 * D)).astype(BF)


def pack_first(w_qkv, *vectors):
    vmem = pl.BlockSpec(memory_space=pltpu.VMEM)
    return pl.pallas_call(
        pack_kernel,
        in_specs=[vmem] * (1 + len(vectors)),
        out_specs=vmem,
        out_shape=pltpu.HBM((HD + EXTRA, 3 * D), BF),
        name="pack_first",
    )(w_qkv, *[v.reshape(1, -1) for v in vectors])


def project_kernel(at_ref, x_ref, *refs):
    pieces, (out_ref, vec_ref, bup_ref, full_ref, w, small, sems) = refs[:16], refs[16:]
    copies = []
    for k, (piece, s) in enumerate(zip(pieces, owners(at_ref))):
        copies.append(
            pltpu.make_async_copy(piece.at[pl.ds(HD, EXTRA), pl.ds(0, D)], small.at[s], sems.at[1, k])
        )
        copies.append(pltpu.make_async_copy(piece.at[pl.ds(0, HD)], w.at[s], sems.at[0, k]))
    for copy in copies:
        copy.start()
    for copy in copies:
        copy.wait()
    back = pltpu.make_async_copy(w, full_ref, sems.at[0, 0])
    back.start()
    rows = [small[s].astype(F32)[:1] for s in range(16)]
    for k in range(8):
        vec_ref[k : k + 1] = jnp.concatenate([r[:, k * HD : (k + 1) * HD] for r in rows], axis=1)
    bup_ref[...] = jnp.concatenate([r[:, 8 * HD : 8 * HD + 256] for r in rows], axis=1)
    x = x_ref[...]
    wide = 2 * LANES
    for part in range(3):
        for b in range(D // wide):
            cols = slice(part * D + b * wide, part * D + (b + 1) * wide)
            value = dot(x, w[:, :, cols].reshape(D, wide))
            if part != 1:
                row = 0 if part == 0 else 1
                value = value + vec_ref[row : row + 1, b * wide : (b + 1) * wide]
            low = value.astype(BF)
            out_ref[2 * b, part] = low[:, :LANES]
            out_ref[2 * b + 1, part] = low[:, LANES:]
    back.wait()


def project(at, x, pieces):
    vmem = pl.BlockSpec(memory_space=pltpu.VMEM)
    hbm = pl.BlockSpec(memory_space=pltpu.HBM)
    return pl.pallas_call(
        project_kernel,
        in_specs=[pl.BlockSpec(memory_space=pltpu.SMEM), vmem] + [hbm] * 16,
        out_specs=[vmem] * 3 + [hbm],
        out_shape=[
            jax.ShapeDtypeStruct((PAIRS, 3, ROWS, LANES), BF),
            jax.ShapeDtypeStruct((8, D), F32),
            jax.ShapeDtypeStruct((1, FF), F32),
            pltpu.HBM((16, HD, 3 * D), BF),
        ],
        scratch_shapes=[
            pltpu.VMEM((16, HD, 3 * D), BF),
            pltpu.VMEM((16, EXTRA, D), BF),
            pltpu.SemaphoreType.DMA((2, 16)),
        ],
        compiler_params=pltpu.CompilerParams(vmem_limit_bytes=VMEM_LIMIT),
        cost_estimate=cost(
            flops=6 * ROWS * D * D, bytes_accessed=8 * D * D, transcendentals=0
        ),
        name="project",
    )(at, x, *pieces)


def attend_kernel(q_ref, k_ref, v_ref, low_ref, full_ref, lse_ref):
    q = q_ref[...] * jnp.asarray(HD**-0.5, BF)
    k = k_ref[...].reshape(-1, LANES)
    v = v_ref[...].reshape(-1, LANES)
    lane = lax.broadcasted_iota(jnp.int32, q.shape, 1)
    outs, logs = [], []
    for h in range(2):
        mine = (lane < HD) if h == 0 else (lane >= HD)
        scores = dot(jnp.where(mine, q, jnp.zeros_like(q)), k, NT)
        peak = jnp.max(scores, axis=1, keepdims=True)
        expo = jnp.exp(scores - peak)
        total = jnp.sum(expo, axis=1, keepdims=True)
        outs.append(dot(expo.astype(BF), v) / total)
        logs.append(peak + jnp.log(total))
    out = jnp.where(lane < HD, outs[0], outs[1])
    full_ref[...] = out
    low_ref[...] = out.astype(BF)
    lse_ref[...] = jnp.where(lane < HD, logs[0], logs[1])


def part_specs():
    block = pl.BlockSpec((None, None, ROWS, LANES), lambda i: (i, 0, 0, 0))
    keys = pl.BlockSpec((PAIRS, None, ROWS, LANES), lambda i: (0, 1, 0, 0))
    values = pl.BlockSpec((PAIRS, None, ROWS, LANES), lambda i: (0, 2, 0, 0))
    return [block, keys, values]


def attend(qkv):
    rows = pl.BlockSpec((None, ROWS, LANES), lambda i: (i, 0, 0))
    shape = (PAIRS, ROWS, LANES)
    n = PAIRS * ROWS
    return pl.pallas_call(
        attend_kernel,
        grid=(PAIRS,),
        in_specs=part_specs(),
        out_specs=[rows, rows, rows],
        out_shape=[
            jax.ShapeDtypeStruct(shape, BF),
            jax.ShapeDtypeStruct(shape, F32),
            jax.ShapeDtypeStruct(shape, F32),
        ],
        compiler_params=pltpu.CompilerParams(vmem_limit_bytes=VMEM_LIMIT),
        cost_estimate=cost(
            flops=16 * n * n * LANES, bytes_accessed=16 * n * LANES, transcendentals=2 * n * n
        ),
        name="attend",
    )(qkv, qkv, qkv)


def reflect_kernel(q_ref, k_ref, v_ref, do_ref, o_ref, lse_ref, out_ref, dk_acc, dv_acc):
    i = pl.program_id(0)

    @pl.when(i == 0)
    def _():
        dk_acc[...] = jnp.zeros_like(dk_acc)
        dv_acc[...] = jnp.zeros_like(dv_acc)

    q = q_ref[...] * jnp.asarray(HD**-0.5, BF)
    do = do_ref[...]
    k = k_ref[...].reshape(-1, LANES)
    v = v_ref[...].reshape(-1, LANES)
    lane = lax.broadcasted_iota(jnp.int32, q.shape, 1)
    product = (do.astype(F32) * o_ref[...]).T
    logs = lse_ref[...].T
    dqs, dk, dv = [], None, None
    for h in range(2):
        mine = (lane < HD) if h == 0 else (lane >= HD)
        qh = jnp.where(mine, q, jnp.zeros_like(q))
        doh = jnp.where(mine, do, jnp.zeros_like(do))
        delta = jnp.sum(product[h * HD : (h + 1) * HD], axis=0, keepdims=True)
        probs = jnp.exp(dot(k, qh, NT) - logs[h * HD : h * HD + 1])
        dscores = (probs * (dot(v, doh, NT) - delta)).astype(BF)
        value_part = dot(probs.astype(BF), doh)
        key_part = dot(dscores, qh)
        dv = value_part if dv is None else dv + value_part
        dk = key_part if dk is None else dk + key_part
        dqs.append(dot(dscores, k, TN))
    dk_acc[...] += dk
    dv_acc[...] += dv
    out_ref[i, 0] = (jnp.where(lane < HD, dqs[0], dqs[1]) * HD**-0.5).astype(BF)

    @pl.when(i == PAIRS - 1)
    def _():
        out_ref[:, 1] = dk_acc[...].astype(BF).reshape(PAIRS, ROWS, LANES)
        out_ref[:, 2] = dv_acc[...].astype(BF).reshape(PAIRS, ROWS, LANES)


def reflect(qkv, dattended, attended, logs):
    rows = pl.BlockSpec((None, ROWS, LANES), lambda i: (i, 0, 0))
    n = PAIRS * ROWS
    return pl.pallas_call(
        reflect_kernel,
        grid=(PAIRS,),
        in_specs=part_specs() + [rows, rows, rows],
        out_specs=whole((PAIRS, 3, ROWS, LANES)),
        out_shape=jax.ShapeDtypeStruct((PAIRS, 3, ROWS, LANES), BF),
        scratch_shapes=[pltpu.VMEM((n, LANES), F32)] * 2,
        compiler_params=pltpu.CompilerParams(vmem_limit_bytes=VMEM_LIMIT),
        cost_estimate=cost(
            flops=30 * n * n * LANES, bytes_accessed=20 * n * LANES, transcendentals=2 * n * n
        ),
        name="reflect",
    )(qkv, qkv, qkv, dattended, attended, logs)


ACT, ATT, DFFN, DATTN = 0, FF, FF + D, FF + 2 * D
DPRE, FIRST = 0, FF
PACK_A = (ROWS, FF + 3 * D)
PACK_B = (ROWS + 32, FF + D)
TILE = 512
SMALLS = 6
SMALL = D + SMALLS * 256


def by_group(value, width):
    cut = [value[:, i * width : (i + 1) * width] for i in range(16)]
    return jnp.concatenate([cut[x * 4 + g] for g in range(4) for x in range(4)], axis=1)


def normalize(hidden):
    centered = hidden - jnp.mean(hidden, axis=-1, keepdims=True)
    deviation = lax.rsqrt(jnp.mean(centered * centered, axis=-1, keepdims=True) + ln_epsilon)
    return centered * deviation, deviation


def norm_back(upstream, normal, deviation, gain):
    scaled = upstream * gain
    return deviation * (
        scaled
        - jnp.mean(scaled, axis=-1, keepdims=True)
        - normal * jnp.mean(scaled * normal, axis=-1, keepdims=True)
    )


def column_sum(value):
    return jnp.sum(value, axis=0, keepdims=True)


def feed_kernel(
    at_ref, x_ref, cot_ref, att_ref, vec_ref, bup_ref, *refs
):
    pieces = refs[:16]
    out_ref, dmixed_ref, datt_ref, pack_a, pack_b = refs[16:21]
    feed_body(
        owners(at_ref), pieces, x_ref, cot_ref, att_ref, vec_ref, bup_ref,
        out_ref, dmixed_ref, datt_ref, pack_a, pack_b, *refs[21:],
    )


def feed_body(
    places, pieces, x_ref, cot_ref, att_ref, vec_ref, bup_ref,
    out_ref, dmixed_ref, datt_ref, pack_a, pack_b,
    wout, wup, wdown, first, low_first, normal1, slope, total, bias_sum, sems,
):
    outs, ups, downs = [], [], []
    for k, (piece, s) in enumerate(zip(pieces, places)):
        outs.append(pltpu.make_async_copy(piece.at[0], wout.at[s], sems.at[0, k]))
        ups.append(pltpu.make_async_copy(piece.at[pl.ds(1, 4)], wup.at[:, s], sems.at[1, k]))
        downs.append(pltpu.make_async_copy(piece.at[pl.ds(5, 4)], wdown.at[s], sems.at[2, k]))
    for copy in outs + ups + downs:
        copy.start()

    bias_out, gain1, shift1 = vec_ref[2:3], vec_ref[3:4], vec_ref[4:5]
    bias_down, gain2, shift2 = vec_ref[5:6], vec_ref[6:7], vec_ref[7:8]
    att = jnp.concatenate([att_ref[j] for j in range(PAIRS)], axis=1)
    pack_a[:, ATT : ATT + D] = by_group(att, HD)
    for copy in outs:
        copy.wait()
    mixed = x_ref[...].astype(F32) + dot(att, wout[...].reshape(D, D)) + bias_out
    n1, r1 = normalize(mixed)
    normal1[...] = n1
    value = n1 * gain1 + shift1
    first[...] = value
    first_low = value.astype(BF)
    low_first[...] = first_low
    pack_b[:ROWS, FIRST : FIRST + D] = by_group(first_low, HD)

    total[...] = value + bias_down
    for copy in ups:
        copy.wait()

    def up_tile(u):
        part = pl.ds(pl.multiple_of(u % 2 * TILE, TILE), TILE)
        return wup[u // 2, :, :, part].reshape(D, TILE)

    def down_tile(u):
        return wdown[pl.ds(u * 2, 2)].reshape(TILE, D)

    @pl.loop(0, FF // TILE)
    def _(u):
        cols = pl.ds(pl.multiple_of(u * TILE, TILE), TILE)
        pre = dot(low_first[...], up_tile(u)) + bup_ref[:, cols]
        cdf = 0.5 * (1.0 + lax.erf(pre * 0.7071067811865476))
        slope[:, cols] = cdf + pre * (jnp.exp(-0.5 * pre * pre) * 0.3989422804014327)
        act = (pre * cdf).astype(BF)
        pack_a[:, cols] = act

    for copy in downs:
        copy.wait()

    @pl.loop(0, FF // D)
    def _(u):
        cols = pl.ds(pl.multiple_of(u * D, D), D)
        total[...] += dot(pack_a[:, cols], wdown[pl.ds(u * 4, 4)].reshape(D, D))

    n2, r2 = normalize(total[...])
    out_ref[...] = (n2 * gain2 + shift2).astype(BF)
    dy = cot_ref[...].astype(F32)
    sums = [None] * SMALLS
    sums[4] = column_sum(dy * n2)
    sums[5] = column_sum(dy)
    dffn = norm_back(dy, n2, r2, gain2)
    dffn_low = dffn.astype(BF)
    pack_a[:, DFFN : DFFN + D] = dffn_low
    sums[3] = column_sum(dffn_low.astype(F32))
    total[...] = dffn

    @pl.loop(0, FF // TILE)
    def _(u):
        cols = pl.ds(pl.multiple_of(u * TILE, TILE), TILE)
        grads = dot(pack_a[:, DFFN : DFFN + D], down_tile(u), NT) * slope[:, cols]
        low = grads.astype(BF)
        pack_b[:ROWS, cols] = low
        bias_sum[:, cols] = column_sum(low.astype(F32))
        total[...] += dot(low, up_tile(u), NT)

    dfirst = total[...]
    n1 = normal1[...]
    sums[1] = column_sum(dfirst * n1)
    sums[2] = column_sum(dfirst)
    dmixed = norm_back(dfirst, n1, r1, gain1)
    dmixed_ref[...] = dmixed
    low = dmixed.astype(BF)
    pack_a[:, DATTN : DATTN + D] = low
    sums[0] = column_sum(low.astype(F32))
    sums = [by_group(value, HD) for value in sums]
    ups = by_group(bias_sum[...], 256)
    for g in range(4):
        parts = [ups[:, g * D : (g + 1) * D]] + [v[:, g * 256 : (g + 1) * 256] for v in sums]
        rows = slice(ROWS + g // 2 * 16, ROWS + g // 2 * 16 + 16)
        pack_b[rows, g % 2 * SMALL : (g % 2 + 1) * SMALL] = jnp.broadcast_to(
            jnp.concatenate(parts, axis=1), (16, SMALL)
        ).astype(BF)
    datt = dot(low, wout[...].reshape(D, D), NT).astype(BF)
    for j in range(PAIRS):
        datt_ref[j] = datt[:, j * LANES : (j + 1) * LANES]


def feed(at, x, cotangent, attended, vectors, bias_up, pieces):
    vmem = pl.BlockSpec(memory_space=pltpu.VMEM)
    hbm = pl.BlockSpec(memory_space=pltpu.HBM)
    return pl.pallas_call(
        feed_kernel,
        in_specs=[pl.BlockSpec(memory_space=pltpu.SMEM)] + [vmem] * 5 + [hbm] * 16,
        out_specs=[vmem] * 5,
        out_shape=[
            jax.ShapeDtypeStruct((ROWS, D), BF),
            jax.ShapeDtypeStruct((ROWS, D), F32),
            jax.ShapeDtypeStruct((PAIRS, ROWS, LANES), BF),
            pltpu.HBM(PACK_A, BF),
            pltpu.HBM(PACK_B, BF),
        ],
        scratch_shapes=[
            pltpu.VMEM((16, HD, D), BF),
            pltpu.VMEM((4, 16, HD, D), BF),
            pltpu.VMEM((16, 4, HD, D), BF),
            pltpu.VMEM((ROWS, D), F32),
            pltpu.VMEM((ROWS, D), BF),
            pltpu.VMEM((ROWS, D), F32),
            pltpu.VMEM((ROWS, FF), F32),
            pltpu.VMEM((ROWS, D), F32),
            pltpu.VMEM((1, FF), F32),
            pltpu.SemaphoreType.DMA((3, 16)),
        ],
        compiler_params=pltpu.CompilerParams(vmem_limit_bytes=VMEM_LIMIT),
        cost_estimate=cost(
            flops=40 * ROWS * D * D, bytes_accessed=32 * D * D, transcendentals=2 * ROWS * FF
        ),
        name="feed",
    )(at, x, cotangent, attended, vectors, bias_up, *pieces)


HALF_A = 160
HALF_B = 144


def slot_of(at_ref, x):
    return lax.rem(x + 4 - at_ref[0], 4)


def both_cores(own, far):
    return jnp.concatenate([own[...], far[...]], axis=0)


def grads_a_kernel(at_ref, *refs):
    step = pl.program_id(0)
    act_other, act, att_other, att, dffn, dattn = (
        both_cores(*pair) for pair in zip(refs[:6], refs[6:12])
    )
    outs = (refs[12:14], refs[14:16])
    value = dot(jnp.concatenate([act_other, act], axis=1), dffn, TN).astype(BF)
    slot = slot_of(at_ref, step)
    for side, (one, two) in enumerate(outs):
        one[slot, :128] = value[side * 256 : side * 256 + 128]
        two[slot, :128] = value[side * 256 + 128 : side * 256 + 256]

    @pl.when(step == 0)
    def _():
        value = dot(jnp.concatenate([att_other, att], axis=1), dattn, TN).astype(BF)
        for side, (one, two) in enumerate(outs):
            for x in range(4):
                start = side * 256 + x * 64
                one[slot_of(at_ref, x), 128:160] = value[start : start + 32]
                two[slot_of(at_ref, x), 128:160] = value[start + 32 : start + 64]


def grads_b_kernel(at_ref, *refs):
    step = pl.program_id(0)
    first, first_other, dpre, row_own, row_other = (
        both_cores(*pair) for pair in zip(refs[:5], refs[5:10])
    )
    one, two, one_across, two_across = refs[10:]
    value = dot(jnp.concatenate([first, first_other], axis=1), dpre, TN).astype(BF)
    for half, target in enumerate((one, two)):

        @pl.when(step // 2 == half)
        def _():
            start = pl.multiple_of(step % 2 * 64, 64)
            for side in range(2):
                for x in range(4):
                    rows = value[(side * 4 + x) * 64 : (side * 4 + x + 1) * 64]
                    target[slot_of(at_ref, x), side, pl.ds(start, 64)] = rows

    @pl.when(step == 0)
    def _():
        row = lax.broadcasted_iota(jnp.int32, (16, D), 0)
        for side, tail in enumerate((row_own, row_other)):
            tail = tail[:16].astype(F32) + tail[16:].astype(F32)
            for x in range(4):
                parts = [tail[:, x * 256 : (x + 1) * 256]]
                for k in range(SMALLS):
                    start = D + k * 256 + x * HD
                    parts.append(tail[:, start : start + HD])
                parts.append(jnp.zeros((16, D - 256 - SMALLS * HD), F32))
                value = jnp.where(row == 0, jnp.concatenate(parts, axis=1), 0.0)
                one[slot_of(at_ref, x), side, 128:144] = value.astype(BF)
                two[slot_of(at_ref, x), side, 128:144] = jnp.zeros((16, D), BF)

    @pl.when(step == 3)
    def _():
        one_across[...] = one[2]
        two_across[...] = two[2]


def columns(width, where):
    return pl.BlockSpec((ROWS, width), lambda i, at: (0, where(i, at)))


def small_row(where):
    return pl.BlockSpec(
        (16, SMALL), lambda i, at: (ROWS // 16 + lax.div(where(at), 2), lax.rem(where(at), 2))
    )


def grads(kernel, specs, shapes, name, at, pack, far_pack):
    return pl.pallas_call(
        kernel,
        grid_spec=pltpu.PrefetchScalarGridSpec(
            num_scalar_prefetch=1,
            grid=(4,),
            in_specs=specs + specs,
            out_specs=[whole(shape) for shape in shapes],
        ),
        out_shape=[pltpu.HBM(shape, BF) for shape in shapes],
        compiler_params=pltpu.CompilerParams(vmem_limit_bytes=VMEM_LIMIT),
        cost_estimate=cost(
            flops=6 * ROWS * D * D, bytes_accessed=12 << 20, transcendentals=0
        ),
        name=name,
    )(at, *([pack] * len(specs)), *([far_pack] * len(specs)))


def grads_a(at, pack, far_pack):
    specs = [
        columns(256, lambda i, at: i * 4 + at[2]),
        columns(256, lambda i, at: i * 4 + at[1]),
        columns(256, lambda i, at: ATT // 256 + at[2]),
        columns(256, lambda i, at: ATT // 256 + at[1]),
        columns(D, lambda i, at: DFFN // D),
        columns(D, lambda i, at: DATTN // D),
    ]
    return grads(grads_a_kernel, specs, [(4, HALF_A, D)] * 4, "grads_a", at, pack, far_pack)


def grads_b(at, pack, far_pack):
    specs = [
        columns(256, lambda i, at: FIRST // 256 + at[1]),
        columns(256, lambda i, at: FIRST // 256 + at[2]),
        columns(D, lambda i, at: DPRE // D + i),
        small_row(lambda at: at[1]),
        small_row(lambda at: at[2]),
    ]
    shapes = [(4, 2, HALF_B, D)] * 2 + [(2, HALF_B, D)] * 2
    return grads(grads_b_kernel, specs, shapes, "grads_b", at, pack, far_pack)


def grads_qkv_kernel(x_ref, g_ref, out_ref, total, sums):
    step = pl.program_id(0)

    @pl.when(step == 0)
    def _():
        total[...] = jnp.zeros_like(total)
        sums[...] = jnp.zeros_like(sums)

    both = jnp.concatenate([g_ref[part] for part in range(3)], axis=1)
    total[...] += dot(both, x_ref[...], TN)
    sums[...] += jnp.broadcast_to(column_sum(both.astype(F32)), sums.shape)

    @pl.when(step == PAIRS - 1)
    def _():
        tail = jnp.concatenate([sums[...], jnp.zeros((8, D - 3 * LANES), F32)], axis=1)
        for s in range(16):
            value = total[:, pl.ds(s // 2 * LANES, LANES)].T[s % 2 * HD : (s % 2 + 1) * HD]
            rows = [
                jnp.concatenate(
                    [
                        value[g * 8 : (g + 1) * 8, part * LANES : (part + 1) * LANES]
                        for g in range(8)
                    ],
                    axis=1,
                )
                for part in range(3)
            ]
            out_ref[s] = jnp.concatenate(rows + [tail], axis=0).astype(BF)


def grads_qkv(x_all, dqkv):
    wide = 3 * LANES
    return pl.pallas_call(
        grads_qkv_kernel,
        grid=(PAIRS,),
        in_specs=[
            pl.BlockSpec((None, ROWS, D), lambda i: (i, 0, 0)),
            pl.BlockSpec((None, 3, ROWS, LANES), lambda i: (i, 0, 0, 0)),
        ],
        out_specs=whole((16, 32, D)),
        out_shape=jax.ShapeDtypeStruct((16, 32, D), BF),
        scratch_shapes=[pltpu.VMEM((wide, D), F32), pltpu.VMEM((8, wide), F32)],
        compiler_params=pltpu.CompilerParams(vmem_limit_bytes=VMEM_LIMIT),
        cost_estimate=cost(
            flops=6 * ROWS * D * D, bytes_accessed=6 << 20, transcendentals=0
        ),
        name="grads_qkv",
    )(x_all, dqkv)


CHUNK = 80
FLAT = PAIRS * CHUNK


def unpack_kernel(at_ref, total_ref, qkv_ref, out_ref, up_ref, down_ref, bias_up_ref, *small_refs):
    def put(target, start, count, cols=slice(None), first=0):
        while count:
            chunk, row = divmod(start, CHUNK)
            step = min(count, CHUNK - row)
            target[first : first + step, cols] = total_ref[chunk, row : row + step].astype(F32)
            start, count, first = start + step, count - step, first + step

    put(down_ref, 0, 128)
    put(out_ref, 128, 32)
    put(down_ref, HALF_A, 128, first=128)
    put(out_ref, HALF_A + 128, 32, first=32)
    base = 2 * HALF_A
    for block in range(4):
        start = base + block // 2 * HALF_B + block % 2 * 64
        put(up_ref, start, 64, slice(block * D, (block + 1) * D))
    chunk, row = divmod(base + 128, CHUNK)
    tail = total_ref[chunk, row : row + 16].astype(F32)[:1]
    bias_up_ref[...] = tail[:, :256]
    for k in range(SMALLS):
        small_refs[k][...] = tail[:, 256 + k * HD : 256 + (k + 1) * HD]
    for j in range(PAIRS):
        block = total_ref[j, CHUNK:].astype(F32)
        for part in range(3):
            cols = slice(part * D + j * LANES, part * D + (j + 1) * LANES)
            for g in range(8):
                rows = block[part * 8 : (part + 1) * 8, g * LANES : (g + 1) * LANES]
                qkv_ref[g * 8 : (g + 1) * 8, cols] = rows
    shard = at_ref[0]
    tail = total_ref[lax.div(shard, 2), CHUNK:].astype(F32)[24:25]
    for k, part in ((SMALLS, 0), (SMALLS + 1, 2)):
        start = part * LANES
        small_refs[k][...] = jnp.where(
            lax.rem(shard, 2) == 0,
            tail[:, start : start + HD],
            tail[:, start + HD : start + 2 * HD],
        )


def unpack(at, total):
    vmem = pl.BlockSpec(memory_space=pltpu.VMEM)
    shapes = [(HD, 3 * D), (HD, D), (HD, FF), (256, D), (1, 256)] + [(1, HD)] * (SMALLS + 2)
    return pl.pallas_call(
        unpack_kernel,
        in_specs=[pl.BlockSpec(memory_space=pltpu.SMEM), vmem],
        out_specs=[vmem] * len(shapes),
        out_shape=[jax.ShapeDtypeStruct(shape, F32) for shape in shapes],
        compiler_params=pltpu.CompilerParams(vmem_limit_bytes=VMEM_LIMIT),
        name="unpack",
    )(at, total)


def return_kernel(dmixed_ref, grad_ref, w_ref, out_ref):
    step = pl.program_id(0)
    both = jnp.concatenate([grad_ref[j] for j in range(4)], axis=1)
    value = dot(both, w_ref[...].reshape(D, TILE), NT)

    @pl.when(step == 0)
    def _():
        out_ref[...] = dmixed_ref[...] + value

    @pl.when(step > 0)
    def _():
        out_ref[...] += value


def return_input(dmixed, dqkv, w_qkv):
    steps = D // TILE
    return pl.pallas_call(
        return_kernel,
        grid=(3 * steps,),
        in_specs=[
            whole((ROWS, D)),
            pl.BlockSpec((4, None, ROWS, LANES), lambda i: (i % steps, i // steps, 0, 0)),
            pl.BlockSpec((16, HD, TILE), lambda i: (0, 0, i)),
        ],
        out_specs=whole((ROWS, D)),
        out_shape=jax.ShapeDtypeStruct((ROWS, D), F32),
        compiler_params=pltpu.CompilerParams(vmem_limit_bytes=VMEM_LIMIT),
        cost_estimate=cost(
            flops=6 * ROWS * D * D, bytes_accessed=8 * D * D, transcendentals=0
        ),
        name="return_input",
    )(dmixed, dqkv, w_qkv)


def exchange(array):
    return lax.all_to_all(array, CTX, 0, 0, tiled=True)


def shards(
    inputs, cotangent, w_qkv, bias_query, bias_value, w_out, bias_out, gain_attn, shift_attn,
    w_up, bias_up, w_down, bias_down, gain_ffn, shift_ffn,
):
    tokens = inputs[0]
    where_x = lax.axis_index("x").astype(jnp.int32)
    where_y = lax.axis_index("yl").astype(jnp.int32)
    core = lax.axis_index("core").astype(jnp.int32)
    at = jnp.stack([where_x, where_y, core])
    group, group_other = where_y * 2 + core, (1 - where_y) * 2 + core
    own = jnp.stack([where_x, group, group_other])
    barrier = lax.optimization_barrier

    first_piece = pack_first(
        w_qkv, bias_query, bias_value, bias_out, gain_attn, shift_attn, bias_down, gain_ffn,
        shift_ffn, bias_up,
    )
    two = []
    first_pieces = gather(first_piece, 1, two)
    piece = jnp.concatenate(
        [w_out[None], w_up.reshape(HD, 4, D).transpose(1, 0, 2), w_down.reshape(4, HD, D)], axis=0
    )
    piece, _ = barrier((piece, two[0]))
    first_pieces[7], near = barrier((first_pieces[7], tokens))
    far = move(near, dy=2)
    qkv, vectors, full_bias_up, full_qkv = project(at, tokens, first_pieces)
    qkv, far = barrier((qkv, far))
    both = jnp.where(lax.axis_index("yh") == 0, jnp.stack([tokens, far]), jnp.stack([far, tokens]))
    x_all = lax.all_gather(both, "z", axis=0, tiled=True)
    qkv = exchange(qkv)
    held = []

    def hold(near, *arrays):
        *near, here = barrier((*near, qkv))
        held.extend(attend(here))
        out = barrier((*arrays, held[0]))
        held[0] = out[-1]
        return out[:-1] + tuple(near)

    def hold_last(array):
        array, arrived = barrier((array, exchange(held[0])))
        held.append(arrived)
        return array

    pieces = gather(piece, -1, None, hold, hold_last)
    _, attended, logs, attended_low = held
    outputs, dmixed, dattended, pack_a, pack_b = feed(
        at, tokens, cotangent[0], attended_low, vectors, full_bias_up, pieces
    )
    far_b = move(pack_b, dcore=1)
    pack_a, far_b = barrier((pack_a, far_b))
    far_a = move(pack_a, dcore=1)
    dattended = exchange(dattended)

    *b_halves, one_across, two_across = grads_b(own, pack_b, far_b)
    a_grads = grads_a(own, pack_a, far_a)
    held = []

    def hold_b(*arrays):
        out = barrier((*arrays, a_grads))
        held.append(out[-1])
        return out[:-1]

    b_right, b_left = along_x([(half,) for half in b_halves], hold_b, (one_across, two_across))
    *a_sent, a_kept_one, a_kept_two = a_grads
    a_arrived = tuple(move(a_sent[h], dy=1 - 2 * h) for h in range(2))
    dqkv = reflect(qkv, dattended, attended, logs)
    a_arrived, b_right, b_left, dqkv = barrier((a_arrived, b_right, b_left, dqkv))

    b_sum = [plus(b_halves[h][0], b_right[h], b_left[h]) for h in range(2)]
    b_sum = [
        plus(b_sum[h][0], move(b_sum[h][1], dy=1 - 2 * h)) for h in range(2)
    ]
    a_halves = [(a_kept_one, a_arrived[0]), (a_kept_two, a_arrived[1])]
    part = grads_qkv(x_all, dqkv)


    def hold_a(*arrays):
        out = barrier((*arrays, part))
        held.append(out[-1])
        return out[:-1]

    a_right, a_left = along_x(a_halves, hold_a)
    part = lax.all_to_all(held[-1], SHARD, 0, 0, tiled=True)
    part = jnp.sum(part.astype(F32), axis=0).astype(BF)
    dqkv = exchange(dqkv)
    a_right, a_left, dqkv = barrier((a_right, a_left, dqkv))
    input_grad = return_input(dmixed, dqkv, full_qkv)

    a_sum = [
        plus(*[term[0] for term in a_halves[h]], a_right[h], a_left[h]) for h in range(2)
    ]
    total = jnp.concatenate(a_sum + b_sum + [jnp.zeros((32, D), BF)], axis=0)
    total = exchange(total.reshape(PAIRS, CHUNK, D))
    total = jnp.sum(total.astype(F32), axis=0).astype(BF)
    total = jnp.concatenate([total, part], axis=0)
    total, input_grad = barrier((total, input_grad))
    total = exchange(jnp.broadcast_to(total[None], (PAIRS,) + total.shape))
    shard = where_x * 4 + where_y * 2 + core
    grad_qkv, grad_out, grad_up, grad_down, grad_bias_up, *smalls = unpack(shard[None], total)
    grad_bias_up = grad_bias_up.reshape(256)
    smalls = [v.reshape(HD) for v in smalls]
    mine = (smalls[6], None, smalls[7])
    return (
        outputs[None],
        input_grad[None],
        grad_qkv,
        mine[0],
        mine[2],
        grad_out,
        smalls[0],
        smalls[1],
        smalls[2],
        grad_up,
        grad_bias_up,
        grad_down,
        smalls[3],
        smalls[4],
        smalls[5],
    )


def solution(mesh):
    fine = Mesh(mesh.devices.reshape(4, 2, 4, 2, 2), ALL)
    tokens = P(SHARD, CTX, None)
    matrix = P(SHARD, None)
    vector = P(SHARD)
    parameters = (
        matrix, vector, vector, matrix, vector, vector, vector,
        matrix, vector, matrix, vector, vector, vector,
    )
    return jax.shard_map(
        shards,
        mesh=fine,
        in_specs=(tokens, tokens) + parameters,
        out_specs=(tokens, tokens) + parameters,
        check_vma=False,
    )
```

```python
from functools import partial

import jax
import jax.numpy as jnp
from jax import lax
from jax.experimental import pallas as pl
from jax.experimental.pallas import tpu as pltpu
from jax.sharding import Mesh, PartitionSpec as P

D = 1024
FF = 4096
HEADS = 16
HD = 64
PAIRS = 8
ROWS = 256
LANES = 128
ln_epsilon = 1e-12
VMEM_LIMIT = 60 << 20
SHARE = 1
F32 = jnp.float32
BF = jnp.bfloat16

ALL = ("z", "yh", "x", "yl", "core")
SHARD = ("x", "yl", "core")
CTX = ("z", "yh")

NN = (((1,), (0,)), ((), ()))
NT = (((1,), (1,)), ((), ()))
TN = (((0,), (0,)), ((), ()))


def dot(left, right, dims=NN):
    return lax.dot_general(left, right, dims, preferred_element_type=F32)


def place(z, y, x, core):
    return (((z % 4 * 2 + y % 4 // 2) * 4 + x % 4) * 2 + y % 2) * 2 + core % 2


def move(array, dz=0, dy=0, dx=0, dcore=0):
    pairs = [
        (place(z, y, x, core), place(z + dz, y + dy, x + dx, core + dcore))
        for z in range(4)
        for y in range(4)
        for x in range(4)
        for core in range(2)
    ]
    return lax.ppermute(array, ALL, pairs)


def plus(*terms):
    total = terms[0].astype(F32)
    for term in terms[1:]:
        total = total + term.astype(F32)
    return total.astype(BF)


def gather(piece, way, after_two=None, hold=None, hold_last=None):
    barrier = lax.optimization_barrier
    behind, ahead, side = barrier((move(piece, dx=1), move(piece, dx=-1), move(piece, dy=way)))
    across = move(behind, dx=1)
    side_behind = move(behind, dy=-way)
    side_ahead = move(side, dx=-1)
    near = [move(p, dcore=1) for p in (piece, behind, ahead)]
    if hold is None:
        across, side_behind, side_ahead, *near = barrier((across, side_behind, side_ahead, *near))
        after_two.append(across)
        side_across = move(across, dy=way)
        late = (side, across, side_behind, side_ahead, side_across)
        side, *last = late = barrier(late)
        near += [move(p, dcore=1) for p in late]
    else:
        near.append(move(side, dcore=1))
        side_across = move(across, dy=way)
        side_behind, side_ahead, *near = hold(near, side_behind, side_ahead)
        last = [across, side_behind, side_ahead, side_across]
        near += [move(p, dcore=1) for p in last[:3]]
        near.append(move(hold_last(side_across), dcore=1))
    return [piece, behind, ahead, side] + last + near


FOUND = [
    (x, y, core)
    for core in range(2)
    for x, y in ((0, 0), (3, 0), (1, 0), (0, 1), (2, 0), (3, 1), (1, 1), (2, 1))
]


def owners(at_ref):
    return [
        (lax.rem(at_ref[0] + x, 4) * 2 + lax.rem(at_ref[1] + y, 2)) * 2
        + lax.rem(at_ref[2] + core, 2)
        for x, y, core in FOUND
    ]


def along_x(halves, hold, across=None):
    def slot(half, d, *more):
        return plus(*[term[d] for term in halves[half]], *more)

    across = across or (slot(0, 2), slot(1, 2))
    ahead, behind = hold(move(across[0], dx=1), move(across[1], dx=-1))
    right = move(jnp.stack([slot(0, 1, ahead), slot(1, 1)]), dx=1)
    left = move(jnp.stack([slot(0, 3), slot(1, 3, behind)]), dx=-1)
    return right, left


def cost(flops, bytes_accessed, transcendentals):
    return pl.CostEstimate(
        flops=flops // SHARE,
        bytes_accessed=bytes_accessed // SHARE,
        transcendentals=transcendentals // SHARE,
    )


def whole(shape):
    return pl.BlockSpec(shape, lambda *_: (0,) * len(shape))


EXTRA = 16


def pack_kernel(w_ref, *refs):
    out_ref = refs[-1]
    out_ref[:HD] = w_ref[...]
    parts = [ref[...] for ref in refs[:-1]] + [jnp.zeros((1, 2 * D + 256), BF)]
    row = jnp.concatenate([p.astype(F32) for p in parts], axis=1)
    out_ref[HD:] = jnp.broadcast_to(row, (EXTRA, 3 * D)).astype(BF)


def pack_first(w_qkv, *vectors):
    vmem = pl.BlockSpec(memory_space=pltpu.VMEM)
    return pl.pallas_call(
        pack_kernel,
        in_specs=[vmem] * (1 + len(vectors)),
        out_specs=vmem,
        out_shape=pltpu.HBM((HD + EXTRA, 3 * D), BF),
        name="pack_first",
    )(w_qkv, *[v.reshape(1, -1) for v in vectors])


def project_kernel(at_ref, x_ref, *refs):
    pieces, (out_ref, vec_ref, bup_ref, full_ref, w, small, sems) = refs[:16], refs[16:]
    copies = []
    for k, (piece, s) in enumerate(zip(pieces, owners(at_ref))):
        copies.append(
            pltpu.make_async_copy(piece.at[pl.ds(HD, EXTRA), pl.ds(0, D)], small.at[s], sems.at[1, k])
        )
        copies.append(pltpu.make_async_copy(piece.at[pl.ds(0, HD)], w.at[s], sems.at[0, k]))
    for copy in copies:
        copy.start()
    for copy in copies:
        copy.wait()
    back = pltpu.make_async_copy(w, full_ref, sems.at[0, 0])
    back.start()
    rows = [small[s].astype(F32)[:1] for s in range(16)]
    for k in range(8):
        vec_ref[k : k + 1] = jnp.concatenate([r[:, k * HD : (k + 1) * HD] for r in rows], axis=1)
    bup_ref[...] = jnp.concatenate([r[:, 8 * HD : 8 * HD + 256] for r in rows], axis=1)
    x = x_ref[...]
    wide = 2 * LANES
    for part in range(3):
        for b in range(D // wide):
            cols = slice(part * D + b * wide, part * D + (b + 1) * wide)
            value = dot(x, w[:, :, cols].reshape(D, wide))
            if part != 1:
                row = 0 if part == 0 else 1
                value = value + vec_ref[row : row + 1, b * wide : (b + 1) * wide]
            low = value.astype(BF)
            out_ref[2 * b, part] = low[:, :LANES]
            out_ref[2 * b + 1, part] = low[:, LANES:]
    back.wait()


def project(at, x, pieces):
    vmem = pl.BlockSpec(memory_space=pltpu.VMEM)
    hbm = pl.BlockSpec(memory_space=pltpu.HBM)
    return pl.pallas_call(
        project_kernel,
        in_specs=[pl.BlockSpec(memory_space=pltpu.SMEM), vmem] + [hbm] * 16,
        out_specs=[vmem] * 3 + [hbm],
        out_shape=[
            jax.ShapeDtypeStruct((PAIRS, 3, ROWS, LANES), BF),
            jax.ShapeDtypeStruct((8, D), F32),
            jax.ShapeDtypeStruct((1, FF), F32),
            pltpu.HBM((16, HD, 3 * D), BF),
        ],
        scratch_shapes=[
            pltpu.VMEM((16, HD, 3 * D), BF),
            pltpu.VMEM((16, EXTRA, D), BF),
            pltpu.SemaphoreType.DMA((2, 16)),
        ],
        compiler_params=pltpu.CompilerParams(vmem_limit_bytes=VMEM_LIMIT),
        cost_estimate=cost(
            flops=6 * ROWS * D * D, bytes_accessed=8 * D * D, transcendentals=0
        ),
        name="project",
    )(at, x, *pieces)


def attend_kernel(q_ref, k_ref, v_ref, low_ref, full_ref, lse_ref):
    q = q_ref[...] * jnp.asarray(HD**-0.5, BF)
    k = k_ref[...].reshape(-1, LANES)
    v = v_ref[...].reshape(-1, LANES)
    lane = lax.broadcasted_iota(jnp.int32, q.shape, 1)
    outs, logs = [], []
    for h in range(2):
        mine = (lane < HD) if h == 0 else (lane >= HD)
        scores = dot(jnp.where(mine, q, jnp.zeros_like(q)), k, NT)
        peak = jnp.max(scores, axis=1, keepdims=True)
        expo = jnp.exp(scores - peak)
        total = jnp.sum(expo, axis=1, keepdims=True)
        outs.append(dot(expo.astype(BF), v) / total)
        logs.append(peak + jnp.log(total))
    out = jnp.where(lane < HD, outs[0], outs[1])
    full_ref[...] = out
    low_ref[...] = out.astype(BF)
    lse_ref[...] = jnp.where(lane < HD, logs[0], logs[1])


def part_specs():
    block = pl.BlockSpec((None, None, ROWS, LANES), lambda i: (i, 0, 0, 0))
    keys = pl.BlockSpec((PAIRS, None, ROWS, LANES), lambda i: (0, 1, 0, 0))
    values = pl.BlockSpec((PAIRS, None, ROWS, LANES), lambda i: (0, 2, 0, 0))
    return [block, keys, values]


def attend(qkv):
    rows = pl.BlockSpec((None, ROWS, LANES), lambda i: (i, 0, 0))
    shape = (PAIRS, ROWS, LANES)
    n = PAIRS * ROWS
    return pl.pallas_call(
        attend_kernel,
        grid=(PAIRS,),
        in_specs=part_specs(),
        out_specs=[rows, rows, rows],
        out_shape=[
            jax.ShapeDtypeStruct(shape, BF),
            jax.ShapeDtypeStruct(shape, F32),
            jax.ShapeDtypeStruct(shape, F32),
        ],
        compiler_params=pltpu.CompilerParams(vmem_limit_bytes=VMEM_LIMIT),
        cost_estimate=cost(
            flops=16 * n * n * LANES, bytes_accessed=16 * n * LANES, transcendentals=2 * n * n
        ),
        name="attend",
    )(qkv, qkv, qkv)


def reflect_kernel(q_ref, k_ref, v_ref, do_ref, o_ref, lse_ref, out_ref, dk_acc, dv_acc):
    i = pl.program_id(0)

    @pl.when(i == 0)
    def _():
        dk_acc[...] = jnp.zeros_like(dk_acc)
        dv_acc[...] = jnp.zeros_like(dv_acc)

    q = q_ref[...] * jnp.asarray(HD**-0.5, BF)
    do = do_ref[...]
    k = k_ref[...].reshape(-1, LANES)
    v = v_ref[...].reshape(-1, LANES)
    lane = lax.broadcasted_iota(jnp.int32, q.shape, 1)
    product = (do.astype(F32) * o_ref[...]).T
    logs = lse_ref[...].T
    dqs, dk, dv = [], None, None
    for h in range(2):
        mine = (lane < HD) if h == 0 else (lane >= HD)
        qh = jnp.where(mine, q, jnp.zeros_like(q))
        doh = jnp.where(mine, do, jnp.zeros_like(do))
        delta = jnp.sum(product[h * HD : (h + 1) * HD], axis=0, keepdims=True)
        probs = jnp.exp(dot(k, qh, NT) - logs[h * HD : h * HD + 1])
        dscores = (probs * (dot(v, doh, NT) - delta)).astype(BF)
        value_part = dot(probs.astype(BF), doh)
        key_part = dot(dscores, qh)
        dv = value_part if dv is None else dv + value_part
        dk = key_part if dk is None else dk + key_part
        dqs.append(dot(dscores, k, TN))
    dk_acc[...] += dk
    dv_acc[...] += dv
    out_ref[i, 0] = (jnp.where(lane < HD, dqs[0], dqs[1]) * HD**-0.5).astype(BF)

    @pl.when(i == PAIRS - 1)
    def _():
        out_ref[:, 1] = dk_acc[...].astype(BF).reshape(PAIRS, ROWS, LANES)
        out_ref[:, 2] = dv_acc[...].astype(BF).reshape(PAIRS, ROWS, LANES)


def reflect(qkv, dattended, attended, logs):
    rows = pl.BlockSpec((None, ROWS, LANES), lambda i: (i, 0, 0))
    n = PAIRS * ROWS
    return pl.pallas_call(
        reflect_kernel,
        grid=(PAIRS,),
        in_specs=part_specs() + [rows, rows, rows],
        out_specs=whole((PAIRS, 3, ROWS, LANES)),
        out_shape=jax.ShapeDtypeStruct((PAIRS, 3, ROWS, LANES), BF),
        scratch_shapes=[pltpu.VMEM((n, LANES), F32)] * 2,
        compiler_params=pltpu.CompilerParams(vmem_limit_bytes=VMEM_LIMIT),
        cost_estimate=cost(
            flops=30 * n * n * LANES, bytes_accessed=20 * n * LANES, transcendentals=2 * n * n
        ),
        name="reflect",
    )(qkv, qkv, qkv, dattended, attended, logs)


ACT, ATT, DFFN, DATTN = 0, FF, FF + D, FF + 2 * D
DPRE, FIRST = 0, FF
PACK_A = (ROWS, FF + 3 * D)
PACK_B = (ROWS + 32, FF + D)
TILE = 512
SMALLS = 6
SMALL = D + SMALLS * 256


def by_group(value, width):
    cut = [value[:, i * width : (i + 1) * width] for i in range(16)]
    return jnp.concatenate([cut[x * 4 + g] for g in range(4) for x in range(4)], axis=1)


def normalize(hidden):
    centered = hidden - jnp.mean(hidden, axis=-1, keepdims=True)
    deviation = lax.rsqrt(jnp.mean(centered * centered, axis=-1, keepdims=True) + ln_epsilon)
    return centered * deviation, deviation


def norm_back(upstream, normal, deviation, gain):
    scaled = upstream * gain
    return deviation * (
        scaled
        - jnp.mean(scaled, axis=-1, keepdims=True)
        - normal * jnp.mean(scaled * normal, axis=-1, keepdims=True)
    )


def column_sum(value):
    return jnp.sum(value, axis=0, keepdims=True)


def feed_kernel(
    at_ref, x_ref, cot_ref, att_ref, vec_ref, bup_ref, *refs
):
    pieces = refs[:16]
    out_ref, dmixed_ref, datt_ref, pack_a, pack_b = refs[16:21]
    feed_body(
        owners(at_ref), pieces, x_ref, cot_ref, att_ref, vec_ref, bup_ref,
        out_ref, dmixed_ref, datt_ref, pack_a, pack_b, *refs[21:],
    )


def feed_body(
    places, pieces, x_ref, cot_ref, att_ref, vec_ref, bup_ref,
    out_ref, dmixed_ref, datt_ref, pack_a, pack_b,
    wout, wup, wdown, first, low_first, normal1, slope, total, bias_sum, sems,
):
    outs, ups, downs = [], [], []
    for k, (piece, s) in enumerate(zip(pieces, places)):
        outs.append(pltpu.make_async_copy(piece.at[0], wout.at[s], sems.at[0, k]))
        ups.append(pltpu.make_async_copy(piece.at[pl.ds(1, 4)], wup.at[:, s], sems.at[1, k]))
        downs.append(pltpu.make_async_copy(piece.at[pl.ds(5, 4)], wdown.at[s], sems.at[2, k]))
    for copy in outs + ups + downs:
        copy.start()

    bias_out, gain1, shift1 = vec_ref[2:3], vec_ref[3:4], vec_ref[4:5]
    bias_down, gain2, shift2 = vec_ref[5:6], vec_ref[6:7], vec_ref[7:8]
    att = jnp.concatenate([att_ref[j] for j in range(PAIRS)], axis=1)
    pack_a[:, ATT : ATT + D] = by_group(att, HD)
    for copy in outs:
        copy.wait()
    mixed = x_ref[...].astype(F32) + dot(att, wout[...].reshape(D, D)) + bias_out
    n1, r1 = normalize(mixed)
    normal1[...] = n1
    value = n1 * gain1 + shift1
    first[...] = value
    first_low = value.astype(BF)
    low_first[...] = first_low
    pack_b[:ROWS, FIRST : FIRST + D] = by_group(first_low, HD)

    total[...] = value + bias_down
    for copy in ups:
        copy.wait()

    def up_tile(u):
        part = pl.ds(pl.multiple_of(u % 2 * TILE, TILE), TILE)
        return wup[u // 2, :, :, part].reshape(D, TILE)

    def down_tile(u):
        return wdown[pl.ds(u * 2, 2)].reshape(TILE, D)

    @pl.loop(0, FF // TILE, unroll=4)
    def _(u):
        cols = pl.ds(pl.multiple_of(u * TILE, TILE), TILE)
        pre = dot(low_first[...], up_tile(u)) + bup_ref[:, cols]
        cdf = 0.5 * (1.0 + lax.erf(pre * 0.7071067811865476))
        slope[:, cols] = cdf + pre * (jnp.exp(-0.5 * pre * pre) * 0.3989422804014327)
        act = (pre * cdf).astype(BF)
        pack_a[:, cols] = act

    for copy in downs:
        copy.wait()

    @pl.loop(0, FF // D, unroll=2)
    def _(u):
        cols = pl.ds(pl.multiple_of(u * D, D), D)
        total[...] += dot(pack_a[:, cols], wdown[pl.ds(u * 4, 4)].reshape(D, D))

    n2, r2 = normalize(total[...])
    out_ref[...] = (n2 * gain2 + shift2).astype(BF)
    dy = cot_ref[...].astype(F32)
    sums = [None] * SMALLS
    sums[4] = column_sum(dy * n2)
    sums[5] = column_sum(dy)
    dffn = norm_back(dy, n2, r2, gain2)
    dffn_low = dffn.astype(BF)
    pack_a[:, DFFN : DFFN + D] = dffn_low
    sums[3] = column_sum(dffn_low.astype(F32))
    total[...] = dffn

    @pl.loop(0, FF // TILE, unroll=4)
    def _(u):
        cols = pl.ds(pl.multiple_of(u * TILE, TILE), TILE)
        grads = dot(pack_a[:, DFFN : DFFN + D], down_tile(u), NT) * slope[:, cols]
        low = grads.astype(BF)
        pack_b[:ROWS, cols] = low
        bias_sum[:, cols] = column_sum(low.astype(F32))
        total[...] += dot(low, up_tile(u), NT)

    dfirst = total[...]
    n1 = normal1[...]
    sums[1] = column_sum(dfirst * n1)
    sums[2] = column_sum(dfirst)
    dmixed = norm_back(dfirst, n1, r1, gain1)
    dmixed_ref[...] = dmixed
    low = dmixed.astype(BF)
    pack_a[:, DATTN : DATTN + D] = low
    sums[0] = column_sum(low.astype(F32))
    sums = [by_group(value, HD) for value in sums]
    ups = by_group(bias_sum[...], 256)
    for g in range(4):
        parts = [ups[:, g * D : (g + 1) * D]] + [v[:, g * 256 : (g + 1) * 256] for v in sums]
        rows = slice(ROWS + g // 2 * 16, ROWS + g // 2 * 16 + 16)
        pack_b[rows, g % 2 * SMALL : (g % 2 + 1) * SMALL] = jnp.broadcast_to(
            jnp.concatenate(parts, axis=1), (16, SMALL)
        ).astype(BF)
    datt = dot(low, wout[...].reshape(D, D), NT).astype(BF)
    for j in range(PAIRS):
        datt_ref[j] = datt[:, j * LANES : (j + 1) * LANES]


def feed(at, x, cotangent, attended, vectors, bias_up, pieces):
    vmem = pl.BlockSpec(memory_space=pltpu.VMEM)
    hbm = pl.BlockSpec(memory_space=pltpu.HBM)
    return pl.pallas_call(
        feed_kernel,
        in_specs=[pl.BlockSpec(memory_space=pltpu.SMEM)] + [vmem] * 5 + [hbm] * 16,
        out_specs=[vmem] * 5,
        out_shape=[
            jax.ShapeDtypeStruct((ROWS, D), BF),
            jax.ShapeDtypeStruct((ROWS, D), F32),
            jax.ShapeDtypeStruct((PAIRS, ROWS, LANES), BF),
            pltpu.HBM(PACK_A, BF),
            pltpu.HBM(PACK_B, BF),
        ],
        scratch_shapes=[
            pltpu.VMEM((16, HD, D), BF),
            pltpu.VMEM((4, 16, HD, D), BF),
            pltpu.VMEM((16, 4, HD, D), BF),
            pltpu.VMEM((ROWS, D), F32),
            pltpu.VMEM((ROWS, D), BF),
            pltpu.VMEM((ROWS, D), F32),
            pltpu.VMEM((ROWS, FF), F32),
            pltpu.VMEM((ROWS, D), F32),
            pltpu.VMEM((1, FF), F32),
            pltpu.SemaphoreType.DMA((3, 16)),
        ],
        compiler_params=pltpu.CompilerParams(vmem_limit_bytes=VMEM_LIMIT),
        cost_estimate=cost(
            flops=40 * ROWS * D * D, bytes_accessed=32 * D * D, transcendentals=2 * ROWS * FF
        ),
        name="feed",
    )(at, x, cotangent, attended, vectors, bias_up, *pieces)


HALF_A = 160
HALF_B = 144


def slot_of(at_ref, x):
    return lax.rem(x + 4 - at_ref[0], 4)


def both_cores(own, far):
    return jnp.concatenate([own[...], far[...]], axis=0)


def grads_a_kernel(at_ref, *refs):
    step = pl.program_id(0)
    act_other, act, att_other, att, dffn, dattn = (
        both_cores(*pair) for pair in zip(refs[:6], refs[6:12])
    )
    outs = (refs[12:14], refs[14:16])
    value = dot(jnp.concatenate([act_other, act], axis=1), dffn, TN).astype(BF)
    slot = slot_of(at_ref, step)
    for side, (one, two) in enumerate(outs):
        one[slot, :128] = value[side * 256 : side * 256 + 128]
        two[slot, :128] = value[side * 256 + 128 : side * 256 + 256]

    @pl.when(step == 0)
    def _():
        value = dot(jnp.concatenate([att_other, att], axis=1), dattn, TN).astype(BF)
        for side, (one, two) in enumerate(outs):
            for x in range(4):
                start = side * 256 + x * 64
                one[slot_of(at_ref, x), 128:160] = value[start : start + 32]
                two[slot_of(at_ref, x), 128:160] = value[start + 32 : start + 64]


def grads_b_kernel(at_ref, *refs):
    step = pl.program_id(0)
    first, first_other, dpre, row_own, row_other = (
        both_cores(*pair) for pair in zip(refs[:5], refs[5:10])
    )
    one, two, one_across, two_across = refs[10:]
    value = dot(jnp.concatenate([first, first_other], axis=1), dpre, TN).astype(BF)
    for half, target in enumerate((one, two)):

        @pl.when(step // 2 == half)
        def _():
            start = pl.multiple_of(step % 2 * 64, 64)
            for side in range(2):
                for x in range(4):
                    rows = value[(side * 4 + x) * 64 : (side * 4 + x + 1) * 64]
                    target[slot_of(at_ref, x), side, pl.ds(start, 64)] = rows

    @pl.when(step == 0)
    def _():
        row = lax.broadcasted_iota(jnp.int32, (16, D), 0)
        for side, tail in enumerate((row_own, row_other)):
            tail = tail[:16].astype(F32) + tail[16:].astype(F32)
            for x in range(4):
                parts = [tail[:, x * 256 : (x + 1) * 256]]
                for k in range(SMALLS):
                    start = D + k * 256 + x * HD
                    parts.append(tail[:, start : start + HD])
                parts.append(jnp.zeros((16, D - 256 - SMALLS * HD), F32))
                value = jnp.where(row == 0, jnp.concatenate(parts, axis=1), 0.0)
                one[slot_of(at_ref, x), side, 128:144] = value.astype(BF)
                two[slot_of(at_ref, x), side, 128:144] = jnp.zeros((16, D), BF)

    @pl.when(step == 3)
    def _():
        one_across[...] = one[2]
        two_across[...] = two[2]


def columns(width, where):
    return pl.BlockSpec((ROWS, width), lambda i, at: (0, where(i, at)))


def small_row(where):
    return pl.BlockSpec(
        (16, SMALL), lambda i, at: (ROWS // 16 + lax.div(where(at), 2), lax.rem(where(at), 2))
    )


def grads(kernel, specs, shapes, name, at, pack, far_pack):
    return pl.pallas_call(
        kernel,
        grid_spec=pltpu.PrefetchScalarGridSpec(
            num_scalar_prefetch=1,
            grid=(4,),
            in_specs=specs + specs,
            out_specs=[whole(shape) for shape in shapes],
        ),
        out_shape=[pltpu.HBM(shape, BF) for shape in shapes],
        compiler_params=pltpu.CompilerParams(vmem_limit_bytes=VMEM_LIMIT),
        cost_estimate=cost(
            flops=6 * ROWS * D * D, bytes_accessed=12 << 20, transcendentals=0
        ),
        name=name,
    )(at, *([pack] * len(specs)), *([far_pack] * len(specs)))


def grads_a(at, pack, far_pack):
    specs = [
        columns(256, lambda i, at: i * 4 + at[2]),
        columns(256, lambda i, at: i * 4 + at[1]),
        columns(256, lambda i, at: ATT // 256 + at[2]),
        columns(256, lambda i, at: ATT // 256 + at[1]),
        columns(D, lambda i, at: DFFN // D),
        columns(D, lambda i, at: DATTN // D),
    ]
    return grads(grads_a_kernel, specs, [(4, HALF_A, D)] * 4, "grads_a", at, pack, far_pack)


def grads_b(at, pack, far_pack):
    specs = [
        columns(256, lambda i, at: FIRST // 256 + at[1]),
        columns(256, lambda i, at: FIRST // 256 + at[2]),
        columns(D, lambda i, at: DPRE // D + i),
        small_row(lambda at: at[1]),
        small_row(lambda at: at[2]),
    ]
    shapes = [(4, 2, HALF_B, D)] * 2 + [(2, HALF_B, D)] * 2
    return grads(grads_b_kernel, specs, shapes, "grads_b", at, pack, far_pack)


def grads_qkv_kernel(x_ref, g_ref, out_ref, total, sums):
    step = pl.program_id(0)

    @pl.when(step == 0)
    def _():
        total[...] = jnp.zeros_like(total)
        sums[...] = jnp.zeros_like(sums)

    both = jnp.concatenate([g_ref[part] for part in range(3)], axis=1)
    total[...] += dot(both, x_ref[...], TN)
    sums[...] += jnp.broadcast_to(column_sum(both.astype(F32)), sums.shape)

    @pl.when(step == PAIRS - 1)
    def _():
        tail = jnp.concatenate([sums[...], jnp.zeros((8, D - 3 * LANES), F32)], axis=1)
        for s in range(16):
            value = total[:, pl.ds(s // 2 * LANES, LANES)].T[s % 2 * HD : (s % 2 + 1) * HD]
            rows = [
                jnp.concatenate(
                    [
                        value[g * 8 : (g + 1) * 8, part * LANES : (part + 1) * LANES]
                        for g in range(8)
                    ],
                    axis=1,
                )
                for part in range(3)
            ]
            out_ref[s] = jnp.concatenate(rows + [tail], axis=0).astype(BF)


def grads_qkv(x_all, dqkv):
    wide = 3 * LANES
    return pl.pallas_call(
        grads_qkv_kernel,
        grid=(PAIRS,),
        in_specs=[
            pl.BlockSpec((None, ROWS, D), lambda i: (i, 0, 0)),
            pl.BlockSpec((None, 3, ROWS, LANES), lambda i: (i, 0, 0, 0)),
        ],
        out_specs=whole((16, 32, D)),
        out_shape=jax.ShapeDtypeStruct((16, 32, D), BF),
        scratch_shapes=[pltpu.VMEM((wide, D), F32), pltpu.VMEM((8, wide), F32)],
        compiler_params=pltpu.CompilerParams(vmem_limit_bytes=VMEM_LIMIT),
        cost_estimate=cost(
            flops=6 * ROWS * D * D, bytes_accessed=6 << 20, transcendentals=0
        ),
        name="grads_qkv",
    )(x_all, dqkv)


CHUNK = 80
FLAT = PAIRS * CHUNK


def unpack_kernel(at_ref, total_ref, qkv_ref, out_ref, up_ref, down_ref, bias_up_ref, *small_refs):
    def put(target, start, count, cols=slice(None), first=0):
        while count:
            chunk, row = divmod(start, CHUNK)
            step = min(count, CHUNK - row)
            target[first : first + step, cols] = total_ref[chunk, row : row + step].astype(F32)
            start, count, first = start + step, count - step, first + step

    put(down_ref, 0, 128)
    put(out_ref, 128, 32)
    put(down_ref, HALF_A, 128, first=128)
    put(out_ref, HALF_A + 128, 32, first=32)
    base = 2 * HALF_A
    for block in range(4):
        start = base + block // 2 * HALF_B + block % 2 * 64
        put(up_ref, start, 64, slice(block * D, (block + 1) * D))
    chunk, row = divmod(base + 128, CHUNK)
    tail = total_ref[chunk, row : row + 16].astype(F32)[:1]
    bias_up_ref[...] = tail[:, :256]
    for k in range(SMALLS):
        small_refs[k][...] = tail[:, 256 + k * HD : 256 + (k + 1) * HD]
    for j in range(PAIRS):
        block = total_ref[j, CHUNK:].astype(F32)
        for part in range(3):
            cols = slice(part * D + j * LANES, part * D + (j + 1) * LANES)
            for g in range(8):
                rows = block[part * 8 : (part + 1) * 8, g * LANES : (g + 1) * LANES]
                qkv_ref[g * 8 : (g + 1) * 8, cols] = rows
    shard = at_ref[0]
    tail = total_ref[lax.div(shard, 2), CHUNK:].astype(F32)[24:25]
    for k, part in ((SMALLS, 0), (SMALLS + 1, 2)):
        start = part * LANES
        small_refs[k][...] = jnp.where(
            lax.rem(shard, 2) == 0,
            tail[:, start : start + HD],
            tail[:, start + HD : start + 2 * HD],
        )


def unpack(at, total):
    vmem = pl.BlockSpec(memory_space=pltpu.VMEM)
    shapes = [(HD, 3 * D), (HD, D), (HD, FF), (256, D), (1, 256)] + [(1, HD)] * (SMALLS + 2)
    return pl.pallas_call(
        unpack_kernel,
        in_specs=[pl.BlockSpec(memory_space=pltpu.SMEM), vmem],
        out_specs=[vmem] * len(shapes),
        out_shape=[jax.ShapeDtypeStruct(shape, F32) for shape in shapes],
        compiler_params=pltpu.CompilerParams(vmem_limit_bytes=VMEM_LIMIT),
        name="unpack",
    )(at, total)


def return_kernel(dmixed_ref, grad_ref, w_ref, out_ref):
    step = pl.program_id(0)
    both = jnp.concatenate([grad_ref[j] for j in range(4)], axis=1)
    value = dot(both, w_ref[...].reshape(D, TILE), NT)

    @pl.when(step == 0)
    def _():
        out_ref[...] = dmixed_ref[...] + value

    @pl.when(step > 0)
    def _():
        out_ref[...] += value


def return_input(dmixed, dqkv, w_qkv):
    steps = D // TILE
    return pl.pallas_call(
        return_kernel,
        grid=(3 * steps,),
        in_specs=[
            whole((ROWS, D)),
            pl.BlockSpec((4, None, ROWS, LANES), lambda i: (i % steps, i // steps, 0, 0)),
            pl.BlockSpec((16, HD, TILE), lambda i: (0, 0, i)),
        ],
        out_specs=whole((ROWS, D)),
        out_shape=jax.ShapeDtypeStruct((ROWS, D), F32),
        compiler_params=pltpu.CompilerParams(vmem_limit_bytes=VMEM_LIMIT),
        cost_estimate=cost(
            flops=6 * ROWS * D * D, bytes_accessed=8 * D * D, transcendentals=0
        ),
        name="return_input",
    )(dmixed, dqkv, w_qkv)


def exchange(array):
    return lax.all_to_all(array, CTX, 0, 0, tiled=True)


def shards(
    inputs, cotangent, w_qkv, bias_query, bias_value, w_out, bias_out, gain_attn, shift_attn,
    w_up, bias_up, w_down, bias_down, gain_ffn, shift_ffn,
):
    tokens = inputs[0]
    where_x = lax.axis_index("x").astype(jnp.int32)
    where_y = lax.axis_index("yl").astype(jnp.int32)
    core = lax.axis_index("core").astype(jnp.int32)
    at = jnp.stack([where_x, where_y, core])
    group, group_other = where_y * 2 + core, (1 - where_y) * 2 + core
    own = jnp.stack([where_x, group, group_other])
    barrier = lax.optimization_barrier

    first_piece = pack_first(
        w_qkv, bias_query, bias_value, bias_out, gain_attn, shift_attn, bias_down, gain_ffn,
        shift_ffn, bias_up,
    )
    two = []
    first_pieces = gather(first_piece, 1, two)
    piece = jnp.concatenate(
        [w_out[None], w_up.reshape(HD, 4, D).transpose(1, 0, 2), w_down.reshape(4, HD, D)], axis=0
    )
    piece, _ = barrier((piece, two[0]))
    qkv, vectors, full_bias_up, full_qkv = project(at, tokens, first_pieces)
    qkv = exchange(qkv)
    held = []

    def hold(near, *arrays):
        *near, here = barrier((*near, qkv))
        held.extend(attend(here))
        out = barrier((*arrays, held[0]))
        held[0] = out[-1]
        return out[:-1] + tuple(near)

    def hold_last(array):
        array, arrived = barrier((array, exchange(held[0])))
        held.append(arrived)
        return array

    pieces = gather(piece, -1, None, hold, hold_last)
    _, attended, logs, attended_low = held
    near, attended_low = barrier((tokens, attended_low))
    far = move(near, dy=2)
    outputs, dmixed, dattended, pack_a, pack_b = feed(
        at, tokens, cotangent[0], attended_low, vectors, full_bias_up, pieces
    )
    pack_b, far = barrier((pack_b, far))
    both = jnp.where(lax.axis_index("yh") == 0, jnp.stack([tokens, far]), jnp.stack([far, tokens]))
    x_all = lax.all_gather(both, "z", axis=0, tiled=True)
    far_b = move(pack_b, dcore=1)
    pack_a, far_b = barrier((pack_a, far_b))
    far_a = move(pack_a, dcore=1)
    dattended = exchange(dattended)

    *b_halves, one_across, two_across = grads_b(own, pack_b, far_b)
    a_grads = grads_a(own, pack_a, far_a)
    held = []

    def hold_b(*arrays):
        out = barrier((*arrays, a_grads))
        held.append(out[-1])
        return out[:-1]

    b_right, b_left = along_x([(half,) for half in b_halves], hold_b, (one_across, two_across))
    *a_sent, a_kept_one, a_kept_two = a_grads
    a_arrived = tuple(move(a_sent[h], dy=1 - 2 * h) for h in range(2))
    dqkv = reflect(qkv, dattended, attended, logs)
    a_arrived, b_right, b_left, dqkv = barrier((a_arrived, b_right, b_left, dqkv))

    b_sum = [plus(b_halves[h][0], b_right[h], b_left[h]) for h in range(2)]
    b_sum = [
        plus(b_sum[h][0], move(b_sum[h][1], dy=1 - 2 * h)) for h in range(2)
    ]
    a_halves = [(a_kept_one, a_arrived[0]), (a_kept_two, a_arrived[1])]
    part = grads_qkv(x_all, dqkv)


    def hold_a(*arrays):
        out = barrier((*arrays, part))
        held.append(out[-1])
        return out[:-1]

    a_right, a_left = along_x(a_halves, hold_a)
    part = lax.all_to_all(held[-1], SHARD, 0, 0, tiled=True)
    part = jnp.sum(part.astype(F32), axis=0).astype(BF)
    dqkv = exchange(dqkv)
    a_right, a_left, dqkv = barrier((a_right, a_left, dqkv))
    input_grad = return_input(dmixed, dqkv, full_qkv)

    a_sum = [
        plus(*[term[0] for term in a_halves[h]], a_right[h], a_left[h]) for h in range(2)
    ]
    total = jnp.concatenate(a_sum + b_sum + [jnp.zeros((32, D), BF)], axis=0)
    total = exchange(total.reshape(PAIRS, CHUNK, D))
    total = jnp.sum(total.astype(F32), axis=0).astype(BF)
    total = jnp.concatenate([total, part], axis=0)
    total, input_grad = barrier((total, input_grad))
    total = exchange(jnp.broadcast_to(total[None], (PAIRS,) + total.shape))
    shard = where_x * 4 + where_y * 2 + core
    grad_qkv, grad_out, grad_up, grad_down, grad_bias_up, *smalls = unpack(shard[None], total)
    grad_bias_up = grad_bias_up.reshape(256)
    smalls = [v.reshape(HD) for v in smalls]
    mine = (smalls[6], None, smalls[7])
    return (
        outputs[None],
        input_grad[None],
        grad_qkv,
        mine[0],
        mine[2],
        grad_out,
        smalls[0],
        smalls[1],
        smalls[2],
        grad_up,
        grad_bias_up,
        grad_down,
        smalls[3],
        smalls[4],
        smalls[5],
    )


def solution(mesh):
    fine = Mesh(mesh.devices.reshape(4, 2, 4, 2, 2), ALL)
    tokens = P(SHARD, CTX, None)
    matrix = P(SHARD, None)
    vector = P(SHARD)
    parameters = (
        matrix, vector, vector, matrix, vector, vector, vector,
        matrix, vector, matrix, vector, vector, vector,
    )
    return jax.shard_map(
        shards,
        mesh=fine,
        in_specs=(tokens, tokens) + parameters,
        out_specs=(tokens, tokens) + parameters,
        check_vma=False,
    )
```

```python
from functools import partial

import jax
import jax.numpy as jnp
from jax import lax
from jax.experimental import pallas as pl
from jax.experimental.pallas import tpu as pltpu
from jax.sharding import Mesh, PartitionSpec as P

D = 1024
FF = 4096
HEADS = 16
HD = 64
PAIRS = 8
ROWS = 256
LANES = 128
ln_epsilon = 1e-12
VMEM_LIMIT = 60 << 20
SHARE = 1
F32 = jnp.float32
BF = jnp.bfloat16

ALL = ("z", "yh", "x", "yl", "core")
SHARD = ("x", "yl", "core")
CTX = ("z", "yh")

NN = (((1,), (0,)), ((), ()))
NT = (((1,), (1,)), ((), ()))
TN = (((0,), (0,)), ((), ()))


def dot(left, right, dims=NN):
    return lax.dot_general(left, right, dims, preferred_element_type=F32)


def place(z, y, x, core):
    return (((z % 4 * 2 + y % 4 // 2) * 4 + x % 4) * 2 + y % 2) * 2 + core % 2


def move(array, dz=0, dy=0, dx=0, dcore=0):
    pairs = [
        (place(z, y, x, core), place(z + dz, y + dy, x + dx, core + dcore))
        for z in range(4)
        for y in range(4)
        for x in range(4)
        for core in range(2)
    ]
    return lax.ppermute(array, ALL, pairs)


def plus(*terms):
    total = terms[0].astype(F32)
    for term in terms[1:]:
        total = total + term.astype(F32)
    return total.astype(BF)


def gather(piece, way, after_two=None, hold=None, hold_last=None):
    barrier = lax.optimization_barrier
    behind, ahead, side = barrier((move(piece, dx=1), move(piece, dx=-1), move(piece, dy=way)))
    across = move(behind, dx=1)
    side_behind = move(behind, dy=-way)
    side_ahead = move(side, dx=-1)
    near = [move(p, dcore=1) for p in (piece, behind, ahead)]
    if hold is None:
        across, side_behind, side_ahead, *near = barrier((across, side_behind, side_ahead, *near))
        after_two.append(across)
        side_across = move(across, dy=way)
        late = (side, across, side_behind, side_ahead, side_across)
        side, *last = late = barrier(late)
        near += [move(p, dcore=1) for p in late]
    else:
        near.append(move(side, dcore=1))
        side_across = move(across, dy=way)
        side_behind, side_ahead, *near = hold(near, side_behind, side_ahead)
        last = [across, side_behind, side_ahead, side_across]
        near += [move(p, dcore=1) for p in last[:3]]
        near.append(move(hold_last(side_across), dcore=1))
    return [piece, behind, ahead, side] + last + near


FOUND = [
    (x, y, core)
    for core in range(2)
    for x, y in ((0, 0), (3, 0), (1, 0), (0, 1), (2, 0), (3, 1), (1, 1), (2, 1))
]


def owners(at_ref):
    return [
        (lax.rem(at_ref[0] + x, 4) * 2 + lax.rem(at_ref[1] + y, 2)) * 2
        + lax.rem(at_ref[2] + core, 2)
        for x, y, core in FOUND
    ]


def along_x(halves, hold, across=None):
    def slot(half, d, *more):
        return plus(*[term[d] for term in halves[half]], *more)

    joined = across is not None
    across = across or (slot(0, 2), slot(1, 2))
    ahead, behind = hold(move(across[0], dx=1), move(across[1], dx=-1))
    if joined:
        right, left = join(halves, ahead, behind)
        return move(right, dx=1), move(left, dx=-1)
    right = move(jnp.stack([slot(0, 1, ahead), slot(1, 1)]), dx=1)
    left = move(jnp.stack([slot(0, 3), slot(1, 3, behind)]), dx=-1)
    return right, left


def cost(flops, bytes_accessed, transcendentals):
    return pl.CostEstimate(
        flops=flops // SHARE,
        bytes_accessed=bytes_accessed // SHARE,
        transcendentals=transcendentals // SHARE,
    )


def whole(shape):
    return pl.BlockSpec(shape, lambda *_: (0,) * len(shape))


EXTRA = 16


def pack_kernel(w_ref, *refs):
    out_ref = refs[-1]
    out_ref[:HD] = w_ref[...]
    parts = [ref[...] for ref in refs[:-1]] + [jnp.zeros((1, 2 * D + 256), BF)]
    row = jnp.concatenate([p.astype(F32) for p in parts], axis=1)
    out_ref[HD:] = jnp.broadcast_to(row, (EXTRA, 3 * D)).astype(BF)


def pack_first(w_qkv, *vectors):
    vmem = pl.BlockSpec(memory_space=pltpu.VMEM)
    return pl.pallas_call(
        pack_kernel,
        in_specs=[vmem] * (1 + len(vectors)),
        out_specs=vmem,
        out_shape=pltpu.HBM((HD + EXTRA, 3 * D), BF),
        name="pack_first",
    )(w_qkv, *[v.reshape(1, -1) for v in vectors])


def project_kernel(at_ref, x_ref, *refs):
    pieces, (out_ref, vec_ref, bup_ref, full_ref, w, small, sems) = refs[:16], refs[16:]
    copies = []
    for k, (piece, s) in enumerate(zip(pieces, owners(at_ref))):
        copies.append(
            pltpu.make_async_copy(piece.at[pl.ds(HD, EXTRA), pl.ds(0, D)], small.at[s], sems.at[1, k])
        )
        copies.append(pltpu.make_async_copy(piece.at[pl.ds(0, HD)], w.at[s], sems.at[0, k]))
    for copy in copies:
        copy.start()
    for copy in copies:
        copy.wait()
    back = pltpu.make_async_copy(w, full_ref, sems.at[0, 0])
    back.start()
    rows = [small[s].astype(F32)[:1] for s in range(16)]
    for k in range(8):
        vec_ref[k : k + 1] = jnp.concatenate([r[:, k * HD : (k + 1) * HD] for r in rows], axis=1)
    bup_ref[...] = jnp.concatenate([r[:, 8 * HD : 8 * HD + 256] for r in rows], axis=1)
    x = x_ref[...]
    wide = 2 * LANES
    for part in range(3):
        for b in range(D // wide):
            cols = slice(part * D + b * wide, part * D + (b + 1) * wide)
            value = dot(x, w[:, :, cols].reshape(D, wide))
            if part != 1:
                row = 0 if part == 0 else 1
                value = value + vec_ref[row : row + 1, b * wide : (b + 1) * wide]
            low = value.astype(BF)
            out_ref[2 * b, part] = low[:, :LANES]
            out_ref[2 * b + 1, part] = low[:, LANES:]
    back.wait()


def project(at, x, pieces):
    vmem = pl.BlockSpec(memory_space=pltpu.VMEM)
    hbm = pl.BlockSpec(memory_space=pltpu.HBM)
    return pl.pallas_call(
        project_kernel,
        in_specs=[pl.BlockSpec(memory_space=pltpu.SMEM), vmem] + [hbm] * 16,
        out_specs=[vmem] * 3 + [hbm],
        out_shape=[
            jax.ShapeDtypeStruct((PAIRS, 3, ROWS, LANES), BF),
            jax.ShapeDtypeStruct((8, D), F32),
            jax.ShapeDtypeStruct((1, FF), F32),
            pltpu.HBM((16, HD, 3 * D), BF),
        ],
        scratch_shapes=[
            pltpu.VMEM((16, HD, 3 * D), BF),
            pltpu.VMEM((16, EXTRA, D), BF),
            pltpu.SemaphoreType.DMA((2, 16)),
        ],
        compiler_params=pltpu.CompilerParams(vmem_limit_bytes=VMEM_LIMIT),
        cost_estimate=cost(
            flops=6 * ROWS * D * D, bytes_accessed=8 * D * D, transcendentals=0
        ),
        name="project",
    )(at, x, *pieces)


def attend_kernel(q_ref, k_ref, v_ref, low_ref, full_ref, lse_ref):
    q = q_ref[...] * jnp.asarray(HD**-0.5, BF)
    k = k_ref[...].reshape(-1, LANES)
    v = v_ref[...].reshape(-1, LANES)
    lane = lax.broadcasted_iota(jnp.int32, q.shape, 1)
    outs, logs = [], []
    for h in range(2):
        mine = (lane < HD) if h == 0 else (lane >= HD)
        scores = dot(jnp.where(mine, q, jnp.zeros_like(q)), k, NT)
        peak = jnp.max(scores, axis=1, keepdims=True)
        expo = jnp.exp(scores - peak)
        total = jnp.sum(expo, axis=1, keepdims=True)
        outs.append(dot(expo.astype(BF), v) / total)
        logs.append(peak + jnp.log(total))
    out = jnp.where(lane < HD, outs[0], outs[1])
    full_ref[...] = out
    low_ref[...] = out.astype(BF)
    lse_ref[...] = jnp.where(lane < HD, logs[0], logs[1])


def part_specs():
    block = pl.BlockSpec((None, None, ROWS, LANES), lambda i: (i, 0, 0, 0))
    keys = pl.BlockSpec((PAIRS, None, ROWS, LANES), lambda i: (0, 1, 0, 0))
    values = pl.BlockSpec((PAIRS, None, ROWS, LANES), lambda i: (0, 2, 0, 0))
    return [block, keys, values]


def attend(qkv):
    rows = pl.BlockSpec((None, ROWS, LANES), lambda i: (i, 0, 0))
    shape = (PAIRS, ROWS, LANES)
    n = PAIRS * ROWS
    return pl.pallas_call(
        attend_kernel,
        grid=(PAIRS,),
        in_specs=part_specs(),
        out_specs=[rows, rows, rows],
        out_shape=[
            jax.ShapeDtypeStruct(shape, BF),
            jax.ShapeDtypeStruct(shape, F32),
            jax.ShapeDtypeStruct(shape, F32),
        ],
        compiler_params=pltpu.CompilerParams(vmem_limit_bytes=VMEM_LIMIT),
        cost_estimate=cost(
            flops=16 * n * n * LANES, bytes_accessed=16 * n * LANES, transcendentals=2 * n * n
        ),
        name="attend",
    )(qkv, qkv, qkv)


def reflect_kernel(q_ref, k_ref, v_ref, do_ref, o_ref, lse_ref, out_ref, dk_acc, dv_acc):
    i = pl.program_id(0)

    @pl.when(i == 0)
    def _():
        dk_acc[...] = jnp.zeros_like(dk_acc)
        dv_acc[...] = jnp.zeros_like(dv_acc)

    q = q_ref[...] * jnp.asarray(HD**-0.5, BF)
    do = do_ref[...]
    k = k_ref[...].reshape(-1, LANES)
    v = v_ref[...].reshape(-1, LANES)
    lane = lax.broadcasted_iota(jnp.int32, q.shape, 1)
    product = (do.astype(F32) * o_ref[...]).T
    logs = lse_ref[...].T
    dqs, dk, dv = [], None, None
    for h in range(2):
        mine = (lane < HD) if h == 0 else (lane >= HD)
        qh = jnp.where(mine, q, jnp.zeros_like(q))
        doh = jnp.where(mine, do, jnp.zeros_like(do))
        delta = jnp.sum(product[h * HD : (h + 1) * HD], axis=0, keepdims=True)
        probs = jnp.exp(dot(k, qh, NT) - logs[h * HD : h * HD + 1])
        dscores = (probs * (dot(v, doh, NT) - delta)).astype(BF)
        value_part = dot(probs.astype(BF), doh)
        key_part = dot(dscores, qh)
        dv = value_part if dv is None else dv + value_part
        dk = key_part if dk is None else dk + key_part
        dqs.append(dot(dscores, k, TN))
    dk_acc[...] += dk
    dv_acc[...] += dv
    out_ref[i, 0] = (jnp.where(lane < HD, dqs[0], dqs[1]) * HD**-0.5).astype(BF)

    @pl.when(i == PAIRS - 1)
    def _():
        out_ref[:, 1] = dk_acc[...].astype(BF).reshape(PAIRS, ROWS, LANES)
        out_ref[:, 2] = dv_acc[...].astype(BF).reshape(PAIRS, ROWS, LANES)


def reflect(qkv, dattended, attended, logs):
    rows = pl.BlockSpec((None, ROWS, LANES), lambda i: (i, 0, 0))
    n = PAIRS * ROWS
    return pl.pallas_call(
        reflect_kernel,
        grid=(PAIRS,),
        in_specs=part_specs() + [rows, rows, rows],
        out_specs=whole((PAIRS, 3, ROWS, LANES)),
        out_shape=jax.ShapeDtypeStruct((PAIRS, 3, ROWS, LANES), BF),
        scratch_shapes=[pltpu.VMEM((n, LANES), F32)] * 2,
        compiler_params=pltpu.CompilerParams(vmem_limit_bytes=VMEM_LIMIT),
        cost_estimate=cost(
            flops=30 * n * n * LANES, bytes_accessed=20 * n * LANES, transcendentals=2 * n * n
        ),
        name="reflect",
    )(qkv, qkv, qkv, dattended, attended, logs)


ACT, ATT, DFFN, DATTN = 0, FF, FF + D, FF + 2 * D
DPRE, FIRST = 0, FF
PACK_A = (ROWS, FF + 3 * D)
PACK_B = (ROWS + 32, FF + D)
TILE = 512
SMALLS = 6
SMALL = D + SMALLS * 256


def by_group(value, width):
    cut = [value[:, i * width : (i + 1) * width] for i in range(16)]
    return jnp.concatenate([cut[x * 4 + g] for g in range(4) for x in range(4)], axis=1)


def normalize(hidden):
    centered = hidden - jnp.mean(hidden, axis=-1, keepdims=True)
    deviation = lax.rsqrt(jnp.mean(centered * centered, axis=-1, keepdims=True) + ln_epsilon)
    return centered * deviation, deviation


def norm_back(upstream, normal, deviation, gain):
    scaled = upstream * gain
    return deviation * (
        scaled
        - jnp.mean(scaled, axis=-1, keepdims=True)
        - normal * jnp.mean(scaled * normal, axis=-1, keepdims=True)
    )


def column_sum(value):
    return jnp.sum(value, axis=0, keepdims=True)


def feed_kernel(
    at_ref, x_ref, cot_ref, att_ref, vec_ref, bup_ref, *refs
):
    pieces = refs[:16]
    out_ref, dmixed_ref, datt_ref, pack_a, pack_b = refs[16:21]
    feed_body(
        owners(at_ref), pieces, x_ref, cot_ref, att_ref, vec_ref, bup_ref,
        out_ref, dmixed_ref, datt_ref, pack_a, pack_b, *refs[21:],
    )


def feed_body(
    places, pieces, x_ref, cot_ref, att_ref, vec_ref, bup_ref,
    out_ref, dmixed_ref, datt_ref, pack_a, pack_b,
    wout, wup, wdown, first, low_first, normal1, slope, total, bias_sum, sems,
):
    outs, ups, downs = [], [], []
    for k, (piece, s) in enumerate(zip(pieces, places)):
        outs.append(pltpu.make_async_copy(piece.at[0], wout.at[s], sems.at[0, k]))
        ups.append(pltpu.make_async_copy(piece.at[pl.ds(1, 4)], wup.at[:, s], sems.at[1, k]))
        downs.append(pltpu.make_async_copy(piece.at[pl.ds(5, 4)], wdown.at[s], sems.at[2, k]))
    for copy in outs + ups + downs:
        copy.start()

    bias_out, gain1, shift1 = vec_ref[2:3], vec_ref[3:4], vec_ref[4:5]
    bias_down, gain2, shift2 = vec_ref[5:6], vec_ref[6:7], vec_ref[7:8]
    att = jnp.concatenate([att_ref[j] for j in range(PAIRS)], axis=1)
    pack_a[:, ATT : ATT + D] = by_group(att, HD)
    for copy in outs:
        copy.wait()
    mixed = x_ref[...].astype(F32) + dot(att, wout[...].reshape(D, D)) + bias_out
    n1, r1 = normalize(mixed)
    normal1[...] = n1
    value = n1 * gain1 + shift1
    first[...] = value
    first_low = value.astype(BF)
    low_first[...] = first_low
    pack_b[:ROWS, FIRST : FIRST + D] = by_group(first_low, HD)

    total[...] = value + bias_down
    for copy in ups:
        copy.wait()

    def up_tile(u):
        part = pl.ds(pl.multiple_of(u % 2 * TILE, TILE), TILE)
        return wup[u // 2, :, :, part].reshape(D, TILE)

    def down_tile(u):
        return wdown[pl.ds(u * 2, 2)].reshape(TILE, D)

    @pl.loop(0, FF // TILE, unroll=4)
    def _(u):
        cols = pl.ds(pl.multiple_of(u * TILE, TILE), TILE)
        pre = dot(low_first[...], up_tile(u)) + bup_ref[:, cols]
        cdf = 0.5 * (1.0 + lax.erf(pre * 0.7071067811865476))
        slope[:, cols] = cdf + pre * (jnp.exp(-0.5 * pre * pre) * 0.3989422804014327)
        act = (pre * cdf).astype(BF)
        pack_a[:, cols] = act

    for copy in downs:
        copy.wait()

    @pl.loop(0, FF // D, unroll=2)
    def _(u):
        cols = pl.ds(pl.multiple_of(u * D, D), D)
        total[...] += dot(pack_a[:, cols], wdown[pl.ds(u * 4, 4)].reshape(D, D))

    n2, r2 = normalize(total[...])
    out_ref[...] = (n2 * gain2 + shift2).astype(BF)
    dy = cot_ref[...].astype(F32)
    sums = [None] * SMALLS
    sums[4] = column_sum(dy * n2)
    sums[5] = column_sum(dy)
    dffn = norm_back(dy, n2, r2, gain2)
    dffn_low = dffn.astype(BF)
    pack_a[:, DFFN : DFFN + D] = dffn_low
    sums[3] = column_sum(dffn_low.astype(F32))
    total[...] = dffn

    @pl.loop(0, FF // TILE, unroll=4)
    def _(u):
        cols = pl.ds(pl.multiple_of(u * TILE, TILE), TILE)
        grads = dot(pack_a[:, DFFN : DFFN + D], down_tile(u), NT) * slope[:, cols]
        low = grads.astype(BF)
        pack_b[:ROWS, cols] = low
        bias_sum[:, cols] = column_sum(low.astype(F32))
        total[...] += dot(low, up_tile(u), NT)

    dfirst = total[...]
    n1 = normal1[...]
    sums[1] = column_sum(dfirst * n1)
    sums[2] = column_sum(dfirst)
    dmixed = norm_back(dfirst, n1, r1, gain1)
    dmixed_ref[...] = dmixed
    low = dmixed.astype(BF)
    pack_a[:, DATTN : DATTN + D] = low
    sums[0] = column_sum(low.astype(F32))
    sums = [by_group(value, HD) for value in sums]
    ups = by_group(bias_sum[...], 256)
    for g in range(4):
        parts = [ups[:, g * D : (g + 1) * D]] + [v[:, g * 256 : (g + 1) * 256] for v in sums]
        rows = slice(ROWS + g // 2 * 16, ROWS + g // 2 * 16 + 16)
        pack_b[rows, g % 2 * SMALL : (g % 2 + 1) * SMALL] = jnp.broadcast_to(
            jnp.concatenate(parts, axis=1), (16, SMALL)
        ).astype(BF)
    datt = dot(low, wout[...].reshape(D, D), NT).astype(BF)
    for j in range(PAIRS):
        datt_ref[j] = datt[:, j * LANES : (j + 1) * LANES]


def feed(at, x, cotangent, attended, vectors, bias_up, pieces):
    vmem = pl.BlockSpec(memory_space=pltpu.VMEM)
    hbm = pl.BlockSpec(memory_space=pltpu.HBM)
    return pl.pallas_call(
        feed_kernel,
        in_specs=[pl.BlockSpec(memory_space=pltpu.SMEM)] + [vmem] * 5 + [hbm] * 16,
        out_specs=[vmem] * 5,
        out_shape=[
            jax.ShapeDtypeStruct((ROWS, D), BF),
            jax.ShapeDtypeStruct((ROWS, D), F32),
            jax.ShapeDtypeStruct((PAIRS, ROWS, LANES), BF),
            pltpu.HBM(PACK_A, BF),
            pltpu.HBM(PACK_B, BF),
        ],
        scratch_shapes=[
            pltpu.VMEM((16, HD, D), BF),
            pltpu.VMEM((4, 16, HD, D), BF),
            pltpu.VMEM((16, 4, HD, D), BF),
            pltpu.VMEM((ROWS, D), F32),
            pltpu.VMEM((ROWS, D), BF),
            pltpu.VMEM((ROWS, D), F32),
            pltpu.VMEM((ROWS, FF), F32),
            pltpu.VMEM((ROWS, D), F32),
            pltpu.VMEM((1, FF), F32),
            pltpu.SemaphoreType.DMA((3, 16)),
        ],
        compiler_params=pltpu.CompilerParams(vmem_limit_bytes=VMEM_LIMIT),
        cost_estimate=cost(
            flops=40 * ROWS * D * D, bytes_accessed=32 * D * D, transcendentals=2 * ROWS * FF
        ),
        name="feed",
    )(at, x, cotangent, attended, vectors, bias_up, *pieces)


HALF_A = 160
HALF_B = 144


def slot_of(at_ref, x):
    return lax.rem(x + 4 - at_ref[0], 4)


def both_cores(own, far):
    return jnp.concatenate([own[...], far[...]], axis=0)


def grads_a_kernel(at_ref, *refs):
    step = pl.program_id(0)
    act_other, act, att_other, att, dffn, dattn = (
        both_cores(*pair) for pair in zip(refs[:6], refs[6:12])
    )
    outs = (refs[12:14], refs[14:16])
    value = dot(jnp.concatenate([act_other, act], axis=1), dffn, TN).astype(BF)
    slot = slot_of(at_ref, step)
    for side, (one, two) in enumerate(outs):
        one[slot, :128] = value[side * 256 : side * 256 + 128]
        two[slot, :128] = value[side * 256 + 128 : side * 256 + 256]

    @pl.when(step == 0)
    def _():
        value = dot(jnp.concatenate([att_other, att], axis=1), dattn, TN).astype(BF)
        for side, (one, two) in enumerate(outs):
            for x in range(4):
                start = side * 256 + x * 64
                one[slot_of(at_ref, x), 128:160] = value[start : start + 32]
                two[slot_of(at_ref, x), 128:160] = value[start + 32 : start + 64]


def grads_b_kernel(at_ref, *refs):
    step = pl.program_id(0)
    first, first_other, dpre, row_own, row_other = (
        both_cores(*pair) for pair in zip(refs[:5], refs[5:10])
    )
    one, two, one_across, two_across = refs[10:]
    value = dot(jnp.concatenate([first, first_other], axis=1), dpre, TN).astype(BF)
    for half, target in enumerate((one, two)):

        @pl.when(step // 2 == half)
        def _():
            start = pl.multiple_of(step % 2 * 64, 64)
            for side in range(2):
                for x in range(4):
                    rows = value[(side * 4 + x) * 64 : (side * 4 + x + 1) * 64]
                    target[slot_of(at_ref, x), side, pl.ds(start, 64)] = rows

    @pl.when(step == 0)
    def _():
        row = lax.broadcasted_iota(jnp.int32, (16, D), 0)
        for side, tail in enumerate((row_own, row_other)):
            tail = tail[:16].astype(F32) + tail[16:].astype(F32)
            for x in range(4):
                parts = [tail[:, x * 256 : (x + 1) * 256]]
                for k in range(SMALLS):
                    start = D + k * 256 + x * HD
                    parts.append(tail[:, start : start + HD])
                parts.append(jnp.zeros((16, D - 256 - SMALLS * HD), F32))
                value = jnp.where(row == 0, jnp.concatenate(parts, axis=1), 0.0)
                one[slot_of(at_ref, x), side, 128:144] = value.astype(BF)
                two[slot_of(at_ref, x), side, 128:144] = jnp.zeros((16, D), BF)

    @pl.when(step == 3)
    def _():
        one_across[...] = one[2]
        two_across[...] = two[2]


def columns(width, where):
    return pl.BlockSpec((ROWS, width), lambda i, at: (0, where(i, at)))


def small_row(where):
    return pl.BlockSpec(
        (16, SMALL), lambda i, at: (ROWS // 16 + lax.div(where(at), 2), lax.rem(where(at), 2))
    )


def grads(kernel, specs, shapes, name, at, pack, far_pack):
    return pl.pallas_call(
        kernel,
        grid_spec=pltpu.PrefetchScalarGridSpec(
            num_scalar_prefetch=1,
            grid=(4,),
            in_specs=specs + specs,
            out_specs=[whole(shape) for shape in shapes],
        ),
        out_shape=[pltpu.HBM(shape, BF) for shape in shapes],
        compiler_params=pltpu.CompilerParams(vmem_limit_bytes=VMEM_LIMIT),
        cost_estimate=cost(
            flops=6 * ROWS * D * D, bytes_accessed=12 << 20, transcendentals=0
        ),
        name=name,
    )(at, *([pack] * len(specs)), *([far_pack] * len(specs)))


def grads_a(at, pack, far_pack):
    specs = [
        columns(256, lambda i, at: i * 4 + at[2]),
        columns(256, lambda i, at: i * 4 + at[1]),
        columns(256, lambda i, at: ATT // 256 + at[2]),
        columns(256, lambda i, at: ATT // 256 + at[1]),
        columns(D, lambda i, at: DFFN // D),
        columns(D, lambda i, at: DATTN // D),
    ]
    return grads(grads_a_kernel, specs, [(4, HALF_A, D)] * 4, "grads_a", at, pack, far_pack)


def grads_b(at, pack, far_pack):
    specs = [
        columns(256, lambda i, at: FIRST // 256 + at[1]),
        columns(256, lambda i, at: FIRST // 256 + at[2]),
        columns(D, lambda i, at: DPRE // D + i),
        small_row(lambda at: at[1]),
        small_row(lambda at: at[2]),
    ]
    shapes = [(4, 2, HALF_B, D)] * 2 + [(2, HALF_B, D)] * 2
    return grads(grads_b_kernel, specs, shapes, "grads_b", at, pack, far_pack)


def grads_qkv_kernel(at_ref, x_ref, g_ref, out_ref, total, sums):
    step = pl.program_id(0)

    @pl.when(step == 0)
    def _():
        total[...] = jnp.zeros_like(total)
        sums[...] = jnp.zeros_like(sums)

    both = jnp.concatenate([g_ref[part] for part in range(3)], axis=1)
    total[...] += dot(both, x_ref[...], TN)
    sums[...] += jnp.broadcast_to(column_sum(both.astype(F32)), sums.shape)

    @pl.when(step == PAIRS - 1)
    def _():
        tail = jnp.concatenate([sums[...], jnp.zeros((8, D - 3 * LANES), F32)], axis=1)
        for s in range(16):
            value = total[:, pl.ds(s // 2 * LANES, LANES)].T[s % 2 * HD : (s % 2 + 1) * HD]
            rows = [
                jnp.concatenate(
                    [
                        value[g * 8 : (g + 1) * 8, part * LANES : (part + 1) * LANES]
                        for g in range(8)
                    ],
                    axis=1,
                )
                for part in range(3)
            ]
            out_ref[s] = jnp.concatenate(rows + [tail], axis=0).astype(BF)


def grads_qkv(at, x_all, dqkv):
    wide = 3 * LANES
    return pl.pallas_call(
        grads_qkv_kernel,
        grid_spec=pltpu.PrefetchScalarGridSpec(
            num_scalar_prefetch=1,
            grid=(PAIRS,),
            in_specs=[
                pl.BlockSpec(
                    (None, ROWS, D),
                    lambda i, at: (lax.div(i, 2) * 2 + lax.rem(i + at[0], 2), 0, 0),
                ),
                pl.BlockSpec((None, 3, ROWS, LANES), lambda i, at: (i, 0, 0, 0)),
            ],
            out_specs=whole((16, 32, D)),
            scratch_shapes=[pltpu.VMEM((wide, D), F32), pltpu.VMEM((8, wide), F32)],
        ),
        out_shape=jax.ShapeDtypeStruct((16, 32, D), BF),
        compiler_params=pltpu.CompilerParams(vmem_limit_bytes=VMEM_LIMIT),
        cost_estimate=cost(
            flops=6 * ROWS * D * D, bytes_accessed=6 << 20, transcendentals=0
        ),
        name="grads_qkv",
    )(at, x_all, dqkv)


def join_kernel(count, *refs):
    terms, (ahead, behind, right, left) = refs[: 4 * count], refs[4 * count :]

    def total(k, *more):
        values = [ref[...].astype(F32) for ref in terms[k * count : (k + 1) * count] + more]
        out = values[0]
        for value in values[1:]:
            out = out + value
        return out.astype(BF)

    right[0] = total(0, ahead)
    right[1] = total(1)
    left[0] = total(2)
    left[1] = total(3, behind)


def join(halves, ahead, behind):
    vmem = pl.BlockSpec(memory_space=pltpu.VMEM)
    shape = ahead.shape
    zeros = (0,) * len(shape)

    def slot(d):
        return pl.BlockSpec((None,) + shape, lambda i: (d,) + zeros)

    specs, arrays = [], []
    for d in (1, 3):
        for half in halves:
            specs += [slot(d)] * len(half)
            arrays += list(half)
    both = (2,) + shape
    return pl.pallas_call(
        partial(join_kernel, len(halves[0])),
        grid=(1,),
        in_specs=specs + [whole(shape)] * 2,
        out_specs=[whole(both)] * 2,
        out_shape=[pltpu.HBM(both, BF)] * 2,
        compiler_params=pltpu.CompilerParams(vmem_limit_bytes=VMEM_LIMIT),
        cost_estimate=cost(flops=1 << 20, bytes_accessed=6 << 20, transcendentals=0),
        name="join",
    )(*arrays, ahead, behind)


CHUNK = 80
FLAT = PAIRS * CHUNK


def unpack_kernel(at_ref, total_ref, qkv_ref, out_ref, up_ref, down_ref, bias_up_ref, *small_refs):
    def put(target, start, count, cols=slice(None), first=0):
        while count:
            chunk, row = divmod(start, CHUNK)
            step = min(count, CHUNK - row)
            target[first : first + step, cols] = total_ref[chunk, row : row + step].astype(F32)
            start, count, first = start + step, count - step, first + step

    put(down_ref, 0, 128)
    put(out_ref, 128, 32)
    put(down_ref, HALF_A, 128, first=128)
    put(out_ref, HALF_A + 128, 32, first=32)
    base = 2 * HALF_A
    for block in range(4):
        start = base + block // 2 * HALF_B + block % 2 * 64
        put(up_ref, start, 64, slice(block * D, (block + 1) * D))
    chunk, row = divmod(base + 128, CHUNK)
    tail = total_ref[chunk, row : row + 16].astype(F32)[:1]
    bias_up_ref[...] = tail[:, :256]
    for k in range(SMALLS):
        small_refs[k][...] = tail[:, 256 + k * HD : 256 + (k + 1) * HD]
    for j in range(PAIRS):
        block = total_ref[j, CHUNK:].astype(F32)
        for part in range(3):
            cols = slice(part * D + j * LANES, part * D + (j + 1) * LANES)
            for g in range(8):
                rows = block[part * 8 : (part + 1) * 8, g * LANES : (g + 1) * LANES]
                qkv_ref[g * 8 : (g + 1) * 8, cols] = rows
    shard = at_ref[0]
    tail = total_ref[lax.div(shard, 2), CHUNK:].astype(F32)[24:25]
    for k, part in ((SMALLS, 0), (SMALLS + 1, 2)):
        start = part * LANES
        small_refs[k][...] = jnp.where(
            lax.rem(shard, 2) == 0,
            tail[:, start : start + HD],
            tail[:, start + HD : start + 2 * HD],
        )


def unpack(at, total):
    vmem = pl.BlockSpec(memory_space=pltpu.VMEM)
    shapes = [(HD, 3 * D), (HD, D), (HD, FF), (256, D), (1, 256)] + [(1, HD)] * (SMALLS + 2)
    return pl.pallas_call(
        unpack_kernel,
        in_specs=[pl.BlockSpec(memory_space=pltpu.SMEM), vmem],
        out_specs=[vmem] * len(shapes),
        out_shape=[jax.ShapeDtypeStruct(shape, F32) for shape in shapes],
        compiler_params=pltpu.CompilerParams(vmem_limit_bytes=VMEM_LIMIT),
        name="unpack",
    )(at, total)


def return_kernel(dmixed_ref, grad_ref, w_ref, out_ref):
    step = pl.program_id(0)
    both = jnp.concatenate([grad_ref[j] for j in range(4)], axis=1)
    value = dot(both, w_ref[...].reshape(D, TILE), NT)

    @pl.when(step == 0)
    def _():
        out_ref[...] = dmixed_ref[...] + value

    @pl.when(step > 0)
    def _():
        out_ref[...] += value


def return_input(dmixed, dqkv, w_qkv):
    steps = D // TILE
    return pl.pallas_call(
        return_kernel,
        grid=(3 * steps,),
        in_specs=[
            whole((ROWS, D)),
            pl.BlockSpec((4, None, ROWS, LANES), lambda i: (i % steps, i // steps, 0, 0)),
            pl.BlockSpec((16, HD, TILE), lambda i: (0, 0, i)),
        ],
        out_specs=whole((ROWS, D)),
        out_shape=jax.ShapeDtypeStruct((ROWS, D), F32),
        compiler_params=pltpu.CompilerParams(vmem_limit_bytes=VMEM_LIMIT),
        cost_estimate=cost(
            flops=6 * ROWS * D * D, bytes_accessed=8 * D * D, transcendentals=0
        ),
        name="return_input",
    )(dmixed, dqkv, w_qkv)


def exchange(array):
    return lax.all_to_all(array, CTX, 0, 0, tiled=True)


def shards(
    inputs, cotangent, w_qkv, bias_query, bias_value, w_out, bias_out, gain_attn, shift_attn,
    w_up, bias_up, w_down, bias_down, gain_ffn, shift_ffn,
):
    tokens = inputs[0]
    where_x = lax.axis_index("x").astype(jnp.int32)
    where_y = lax.axis_index("yl").astype(jnp.int32)
    core = lax.axis_index("core").astype(jnp.int32)
    at = jnp.stack([where_x, where_y, core])
    group, group_other = where_y * 2 + core, (1 - where_y) * 2 + core
    own = jnp.stack([where_x, group, group_other])
    barrier = lax.optimization_barrier

    first_piece = pack_first(
        w_qkv, bias_query, bias_value, bias_out, gain_attn, shift_attn, bias_down, gain_ffn,
        shift_ffn, bias_up,
    )
    two = []
    first_pieces = gather(first_piece, 1, two)
    piece = jnp.concatenate(
        [w_out[None], w_up.reshape(HD, 4, D).transpose(1, 0, 2), w_down.reshape(4, HD, D)], axis=0
    )
    piece, _ = barrier((piece, two[0]))
    qkv, vectors, full_bias_up, full_qkv = project(at, tokens, first_pieces)
    qkv = exchange(qkv)
    held = []

    def hold(near, *arrays):
        *near, here = barrier((*near, qkv))
        held.extend(attend(here))
        out = barrier((*arrays, held[0]))
        held[0] = out[-1]
        return out[:-1] + tuple(near)

    def hold_last(array):
        array, arrived = barrier((array, exchange(held[0])))
        held.append(arrived)
        return array

    pieces = gather(piece, -1, None, hold, hold_last)
    _, attended, logs, attended_low = held
    near, attended_low = barrier((tokens, attended_low))
    far = move(near, dy=2)
    outputs, dmixed, dattended, pack_a, pack_b = feed(
        at, tokens, cotangent[0], attended_low, vectors, full_bias_up, pieces
    )
    pack_b, far = barrier((pack_b, far))
    x_all = lax.all_gather(jnp.stack([tokens, far]), "z", axis=0, tiled=True)
    far_b = move(pack_b, dcore=1)
    pack_a, far_b = barrier((pack_a, far_b))
    far_a = move(pack_a, dcore=1)
    dattended = exchange(dattended)

    *b_halves, one_across, two_across = grads_b(own, pack_b, far_b)
    a_grads = grads_a(own, pack_a, far_a)
    held = []

    def hold_b(*arrays):
        out = barrier((*arrays, a_grads))
        held.append(out[-1])
        return out[:-1]

    b_right, b_left = along_x([(half,) for half in b_halves], hold_b, (one_across, two_across))
    *a_sent, a_kept_one, a_kept_two = a_grads
    a_arrived = tuple(move(a_sent[h], dy=1 - 2 * h) for h in range(2))
    dqkv = reflect(qkv, dattended, attended, logs)
    a_arrived, b_right, b_left, dqkv = barrier((a_arrived, b_right, b_left, dqkv))

    b_sum = [plus(b_halves[h][0], b_right[h], b_left[h]) for h in range(2)]
    b_sum = [
        plus(b_sum[h][0], move(b_sum[h][1], dy=1 - 2 * h)) for h in range(2)
    ]
    a_halves = [(a_kept_one, a_arrived[0]), (a_kept_two, a_arrived[1])]
    part = grads_qkv(lax.axis_index("yh").astype(jnp.int32)[None], x_all, dqkv)


    def hold_a(*arrays):
        out = barrier((*arrays, part))
        held.append(out[-1])
        return out[:-1]

    a_right, a_left = along_x(a_halves, hold_a)
    part = lax.all_to_all(held[-1], SHARD, 0, 0, tiled=True)
    part = jnp.sum(part.astype(F32), axis=0).astype(BF)
    dqkv = exchange(dqkv)
    a_right, a_left, dqkv = barrier((a_right, a_left, dqkv))
    input_grad = return_input(dmixed, dqkv, full_qkv)

    a_sum = [
        plus(*[term[0] for term in a_halves[h]], a_right[h], a_left[h]) for h in range(2)
    ]
    total = jnp.concatenate(a_sum + b_sum + [jnp.zeros((32, D), BF)], axis=0)
    total = exchange(total.reshape(PAIRS, CHUNK, D))
    total = jnp.sum(total.astype(F32), axis=0).astype(BF)
    total = jnp.concatenate([total, part], axis=0)
    total, input_grad = barrier((total, input_grad))
    total = exchange(jnp.broadcast_to(total[None], (PAIRS,) + total.shape))
    shard = where_x * 4 + where_y * 2 + core
    grad_qkv, grad_out, grad_up, grad_down, grad_bias_up, *smalls = unpack(shard[None], total)
    grad_bias_up = grad_bias_up.reshape(256)
    smalls = [v.reshape(HD) for v in smalls]
    mine = (smalls[6], None, smalls[7])
    return (
        outputs[None],
        input_grad[None],
        grad_qkv,
        mine[0],
        mine[2],
        grad_out,
        smalls[0],
        smalls[1],
        smalls[2],
        grad_up,
        grad_bias_up,
        grad_down,
        smalls[3],
        smalls[4],
        smalls[5],
    )


def solution(mesh):
    fine = Mesh(mesh.devices.reshape(4, 2, 4, 2, 2), ALL)
    tokens = P(SHARD, CTX, None)
    matrix = P(SHARD, None)
    vector = P(SHARD)
    parameters = (
        matrix, vector, vector, matrix, vector, vector, vector,
        matrix, vector, matrix, vector, vector, vector,
    )
    return jax.shard_map(
        shards,
        mesh=fine,
        in_specs=(tokens, tokens) + parameters,
        out_specs=(tokens, tokens) + parameters,
        check_vma=False,
    )
```
